512 devices in a mesh: row: 16 (over y, z_hi, core), col: 32 (over z_lo, x).
Axes of the slice: x: 4, y: 4, z: 16 (z_hi: 2, z_lo: 8; z = z_hi * 8 + z_lo), core: 2. Of those that a mesh axis runs over, the one named last changes fastest.
Arguments:
- features: bfloat16 [65536, 128], P(('col', 'row')), may hold values from -6 to 6
- weight: bfloat16 [128, 256], replicated, may hold values from -0.5 to 0.5
- tile_values: bfloat16 [16, 4096, 128, 128], P('row', 'col'), may hold values from -0.078125 to 0.078125
- tile_row: int32 [16, 4096], P('row', 'col'), may hold values from 0 to 31
- tile_col: int32 [16, 4096], P('row', 'col'), may hold values from 0 to 15
- tile_count: int32 [16, 32], P('row', 'col'), may hold values from 16 to 128, as said below
- upstream: bfloat16 [65536, 256], P(('row', 'col')), may hold values from -6 to 6
Outputs:
- activated: bfloat16 [65536, 256], P(('row', 'col'))
- feature_grad: bfloat16 [65536, 128], P(('col', 'row'))
- weight_grad: float32 [128, 256], replicated
The draws below stay inside these ranges and needn't reach their ends.
Inputs may be any that keep to these rules, and one draw needn't show every extreme that they name: `tile_count`: some device has all 128 slots live.
All inputs are finite; a program needn't handle non-finite values.
Results may differ from the reference program's by a relative error of at most 0.03.
Values may be sent and summed in bfloat16 or wider, within the bound.
A program may use at most 64 MiB of HBM per device.

```python
import jax
import jax.numpy as jnp
from jax import lax

F_IN = 128
HID = 256
TILE = 128
ROWS_DEV = 128
TILES = 128
NODES = 65536
RB_TILES = 32
CB_TILES = 16
N_ROW = 16
N_COL = 32


def draw_tile_count(key, part):
    key = jax.random.fold_in(key, 7)
    first, second, third = jax.random.split(key, 3)
    base = jax.random.randint(first, (N_ROW, N_COL), TILES // 8, TILES // 2 + 1)
    chosen = jax.random.randint(second, (), 0, N_ROW * N_COL)
    extra = jax.random.randint(third, (N_ROW, N_COL), 0, 16) == 0
    places = jnp.arange(N_ROW * N_COL, dtype=jnp.int32).reshape(N_ROW, N_COL)
    full = extra | (places == chosen)
    return jnp.where(full, TILES, base).astype(jnp.int32)


def set_ends(result, key, least, top_value):
    longest = result.shape.index(max(result.shape))
    spots = []
    for shift in (0, 1):
        where = [jax.random.randint(jax.random.fold_in(key, axis), (), 0, length) for axis, length in enumerate(result.shape)]
        where[longest] = (where[longest] + shift) % result.shape[longest]
        spots.append(tuple(where))
    return result.at[spots[0]].set(least).at[spots[1]].set(top_value)


def shard_levels(key, extent, cuts, low, largest):
    level = 1.0
    for position, blocks in cuts:
        heights = jax.random.uniform(jax.random.fold_in(jax.random.fold_in(key, 6), position), (blocks,), jnp.float32, low / len(cuts), largest / len(cuts))
        level = level * jnp.repeat(jnp.exp(heights), extent[position] // blocks).reshape((-1,) + (1,) * (len(extent) - 1 - position))
    return level


def scatter_about(rng, extent, spread, reach, cuts=(), held_as=jnp.bfloat16):
    values = spread * jax.random.normal(rng, extent, jnp.float32)
    if cuts:
        values = values * shard_levels(rng, extent, cuts, -0.22, 0.18)
    return jnp.clip(values, -reach, reach).astype(held_as)


def setup_inputs(seed: int = 0) -> dict:
    arg_keys = jax.random.split(jax.random.key(seed), 8)
    return {
        "features": scatter_about(arg_keys[0], (NODES, F_IN), 1.0, 6.0, ((0, 512),)),
        "weight": scatter_about(arg_keys[1], (F_IN, HID), F_IN ** -0.5, 0.5),
        "tile_values": scatter_about(arg_keys[2], (N_ROW, N_COL * TILES, TILE, TILE), (TILES * TILE * TILE // (3 * ROWS_DEV) + 1) ** -0.5, 0.078125, ((0, 16), (1, 32))),
        "tile_row": set_ends(jax.random.randint(arg_keys[3], (N_ROW, N_COL * TILES), 0, RB_TILES), jax.random.fold_in(arg_keys[3], 1), 0, RB_TILES - 1).astype(jnp.int32),
        "tile_col": set_ends(jax.random.randint(arg_keys[4], (N_ROW, N_COL * TILES), 0, CB_TILES), jax.random.fold_in(arg_keys[4], 1), 0, CB_TILES - 1).astype(jnp.int32),
        "tile_count": draw_tile_count(jax.random.fold_in(arg_keys[7], 71), 0),
        "upstream": scatter_about(arg_keys[6], (NODES, HID), 1.0, 6.0, ((0, 512),)),
    }


def block_product(values, source_index, target_index, live_slots, source, target_tiles, transpose):
    picked = source[source_index]
    if transpose:
        product = jnp.einsum("kjt,kjh->kth", values.astype(jnp.float32), picked.astype(jnp.float32))
    else:
        product = jnp.einsum("ktj,kjh->kth", values.astype(jnp.float32), picked.astype(jnp.float32))
    targets = jnp.arange(target_tiles, dtype=jnp.int32)
    selector = ((target_index[None, :] == targets[:, None]) & live_slots[None, :]).astype(jnp.float32)
    total = jnp.dot(selector, product.reshape(product.shape[0], -1), precision=lax.Precision.HIGHEST)
    return total.reshape(target_tiles * product.shape[1], product.shape[2])


def rounded(value):
    return lax.optimization_barrier(value.astype(jnp.bfloat16)).astype(jnp.float32)


def reference(features, weight, tile_values, tile_row, tile_col, tile_count, upstream):
    nodes = features.shape[0]
    row_rows = nodes // N_ROW
    col_rows = nodes // N_COL
    devices = N_ROW * N_COL
    values = tile_values.reshape(devices, TILES, TILE, TILE)
    rows_all = tile_row.reshape(devices, TILES)
    cols_all = tile_col.reshape(devices, TILES)
    counts = tile_count.reshape(devices)
    source = features.reshape(nodes // TILE, TILE, F_IN)

    def forward(total, device):
        row_block = device // N_COL
        col_block = device % N_COL
        live_slots = jnp.arange(TILES, dtype=jnp.int32) < counts[device]
        sources = lax.dynamic_slice_in_dim(source, (col_block * (col_rows // TILE)).astype(jnp.int32), col_rows // TILE, 0)
        partial_value = block_product(values[device], cols_all[device], rows_all[device], live_slots, sources, row_rows // TILE, False)
        start = (row_block * row_rows).astype(jnp.int32)
        current = lax.dynamic_slice_in_dim(total, start, row_rows, 0)
        return lax.dynamic_update_slice_in_dim(total, current + rounded(partial_value), start, 0), None

    total, unused = lax.scan(forward, jnp.zeros((nodes, F_IN), jnp.float32), jnp.arange(devices, dtype=jnp.int32))
    aggregated = total.astype(jnp.bfloat16)
    summed = jnp.dot(aggregated, weight, preferred_element_type=jnp.float32)
    sigma = jax.nn.sigmoid(summed)
    activated = (summed * sigma).astype(jnp.bfloat16)
    slope = sigma * (1.0 + summed * (1.0 - sigma))
    grad_rows = (upstream.astype(jnp.float32) * slope).astype(jnp.bfloat16)
    weight_grad = jnp.dot(aggregated.T, grad_rows, preferred_element_type=jnp.float32) * (1.0 / float(nodes) ** 0.5)
    back_rows = jnp.dot(grad_rows, weight.T, preferred_element_type=jnp.float32).astype(jnp.bfloat16)
    grad_source = back_rows.reshape(nodes // TILE, TILE, F_IN)

    def backward(total, device):
        row_block = device // N_COL
        col_block = device % N_COL
        live_slots = jnp.arange(TILES, dtype=jnp.int32) < counts[device]
        sources = lax.dynamic_slice_in_dim(grad_source, (row_block * (row_rows // TILE)).astype(jnp.int32), row_rows // TILE, 0)
        partial_value = block_product(values[device], rows_all[device], cols_all[device], live_slots, sources, col_rows // TILE, True)
        start = (col_block * col_rows).astype(jnp.int32)
        current = lax.dynamic_slice_in_dim(total, start, col_rows, 0)
        return lax.dynamic_update_slice_in_dim(total, current + rounded(partial_value), start, 0), None

    total_back, unused = lax.scan(backward, jnp.zeros((nodes, F_IN), jnp.float32), jnp.arange(devices, dtype=jnp.int32))
    feature_grad = total_back.astype(jnp.bfloat16)
    return activated, feature_grad, weight_grad
```

```python
import functools
import math

import jax
import jax.numpy as jnp
from jax import lax
from jax.experimental import pallas as pl
from jax.experimental.pallas import tpu as pltpu
from jax.sharding import PartitionSpec as P

MESH = pl.DeviceIdType.MESH
F32 = jnp.float32
BF16 = jnp.bfloat16
T = 128

NX, NZ, NY, NH, NC = 4, 8, 4, 2, 2


def order_tables(target, source, live, bins):
    slots = target.shape[1]
    lane = lax.broadcasted_iota(jnp.int32, (slots, slots), 1)
    sub = lax.broadcasted_iota(jnp.int32, (slots, slots), 0)
    wide = jnp.where(lane < live, jnp.broadcast_to(target, (slots, slots)), bins)
    key = wide * slots + lane
    tall = wide.T
    tall_key = tall * slots + sub
    rank = jnp.sum((tall_key < key).astype(jnp.int32), axis=0, keepdims=True)
    tall_rank = jnp.broadcast_to(rank, (slots, slots)).T
    placed = tall_rank == lane
    tall_source = jnp.broadcast_to(source, (slots, slots)).T
    perm = jnp.sum(jnp.where(placed, sub, 0), axis=0, keepdims=True)
    src = jnp.sum(jnp.where(placed, tall_source, 0), axis=0, keepdims=True)
    place = jnp.sum(jnp.where(placed, tall, 0), axis=0, keepdims=True)
    before = jnp.sum(jnp.where(tall_rank + 1 == lane, tall, 0), axis=0, keepdims=True)
    first = lax.broadcasted_iota(jnp.int32, (1, slots), 1) == 0
    keep = jnp.where((place == before) & jnp.logical_not(first), 1, 0)
    upto = jnp.sum((tall <= lane).astype(jnp.int32), axis=0, keepdims=True)
    here = jnp.sum((tall == lane).astype(jnp.int32), axis=0, keepdims=True)
    last = jnp.where(here > 0, upto - 1, slots)
    return perm, src, keep, last


def kernel(
    scale,
    feat_ref, weight_ref, vals_hbm, row_ref, col_ref, count_ref, up_ref,
    act_ref, fg_ref, wg_ref,
    vals, xbuf, sums, pbuf, rx, zs, rz, bbuf, qpack, rq, ys, ry, zh, rzh,
    wown, rw1, ws2, rw2, ws3, rw3, ws4, rw4, ws5, rw5, wy, wall,
    tabv, tabs,
    local_sem, x_send, x_recv, px_send, px_recv, pz_send, pz_recv, b_send, b_recv,
    qc_send, qc_recv, qy_send, qy_recv, qh_send, qh_recv, w_send, w_recv,
):
    r = lax.axis_index("row")
    c = lax.axis_index("col")
    y, h, core = r // (NH * NC), (r // NC) % NH, r % NC
    z, x = c // NX, c % NX
    slots = vals.shape[0]
    sent = []

    def rowdev(yy, hh, cc):
        return {"row": (yy * NH + hh) * NC + cc, "col": c}

    def coldev(zz, xx):
        return {"row": r, "col": zz * NX + xx}

    def send(src, dst, send_sem, recv_sem, device):
        copy = pltpu.make_async_remote_copy(
            src_ref=src, dst_ref=dst, send_sem=send_sem, recv_sem=recv_sem, device_id=device, device_id_type=MESH
        )
        copy.start()
        sent.append(copy)

    def arrived(dst, recv_sem):
        pltpu.make_async_remote_copy(
            src_ref=dst, dst_ref=dst, send_sem=recv_sem, recv_sem=recv_sem, device_id=rowdev(y, h, 1 - core), device_id_type=MESH
        ).wait_recv()

    barrier = pltpu.get_barrier_semaphore()
    peers = [rowdev(y, h, 1 - core), rowdev(y, 1 - h, core)]
    peers += [rowdev((y + d) % NY, h, core) for d in range(1, NY)]
    peers += [coldev(z, (x + d) % NX) for d in range(1, NX)]
    peers += [coldev((z + d) % NZ, x) for d in range(1, NZ)]
    for peer in peers:
        pl.semaphore_signal(barrier, inc=1, device_id=peer, device_id_type=MESH)
    vals_copy = pltpu.make_async_copy(vals_hbm.at[0], vals, local_sem.at[0])
    vals_copy.start()
    live = count_ref[0, 0]
    forward = order_tables(row_ref[...], col_ref[...], live, NZ * NX)
    for i, table in enumerate(forward):
        tabv[i : i + 1, :] = table
    backward = order_tables(col_ref[...], row_ref[...], live, NY * NH * NC)
    for i, table in enumerate(backward):
        tabv[4 + i : 5 + i, :] = table
    tabs_copy = pltpu.make_async_copy(tabv, tabs, local_sem.at[1])
    tabs_copy.start()
    sums[slots] = jnp.zeros((T, T), BF16)
    xbuf[r] = feat_ref[...]
    pl.semaphore_wait(barrier, len(peers))

    def tile_of(yy, hh, cc):
        return (yy * NH + hh) * NC + cc

    n = [0]

    def share(tile, device):
        send(xbuf.at[tile], xbuf.at[tile], x_send.at[n[0]], x_recv.at[tile], device)
        n[0] += 1

    share(r, rowdev(y, 1 - h, core))
    for d in range(1, NY):
        share(r, rowdev((y + d) % NY, h, core))
    share(r, rowdev(y, h, 1 - core))
    other = tile_of(y, 1 - h, core)
    arrived(xbuf.at[other], x_recv.at[other])
    for d in range(1, NY):
        share(other, rowdev((y + d) % NY, h, core))
    share(other, rowdev(y, h, 1 - core))
    for hh in (h, 1 - h):
        for d in range(1, NY):
            tile = tile_of((y + d) % NY, hh, core)
            arrived(xbuf.at[tile], x_recv.at[tile])
            share(tile, rowdev(y, h, 1 - core))
    for hh in range(NH):
        for yy in range(NY):
            tile = tile_of(yy, hh, 1 - core)
            arrived(xbuf.at[tile], x_recv.at[tile])

    tabs_copy.wait()
    vals_copy.wait()

    def product_scan(base, multiply):
        def body(step, total):
            for u in range(8):
                k = step * 8 + u
                keep = tabs[base + 2, k].astype(F32)
                total = total * keep + multiply(tabs[base, k], tabs[base + 1, k])
                sums[k] = total.astype(BF16)
            return total

        lax.fori_loop(0, slots // 8, body, jnp.zeros((T, T), F32))

    product_scan(0, lambda i, s: jnp.dot(vals[i], xbuf[s], preferred_element_type=F32))

    for o in range(1, NZ + 1):
        zz = (z + o) % NZ
        for xx in range(NX):
            pbuf[xx, zz] = sums[tabs[3, zz * NX + xx]]
        for d in range(1, NX):
            send(
                pbuf.at[(x + d) % NX, zz], rx.at[d - 1, o - 1],
                px_send.at[d - 1, o - 1], px_recv.at[d - 1, o - 1], coldev(z, (x + d) % NX),
            )
    for o in range(1, NZ + 1):
        zz = (z + o) % NZ
        total = pbuf[x, zz].astype(F32)
        for d in range(1, NX):
            arrived(rx.at[d - 1, o - 1], px_recv.at[d - 1, o - 1])
            total += rx[d - 1, o - 1].astype(F32)
        if o < NZ:
            zs[o - 1] = total.astype(BF16)
            send(zs.at[o - 1], rz.at[o - 1], pz_send.at[o - 1], pz_recv.at[o - 1], coldev(zz, x))
    for o in range(1, NZ):
        arrived(rz.at[o - 1], pz_recv.at[o - 1])
        total += rz[o - 1].astype(F32)
    aggregated = total.astype(BF16)

    weight = weight_ref[...]
    summed = jnp.dot(aggregated, weight, preferred_element_type=F32)
    sigma = jax.nn.sigmoid(summed)
    slope = sigma * (1.0 + summed * (1.0 - sigma))
    grad_rows = (up_ref[...].astype(F32) * slope).astype(BF16)
    back = lax.dot_general(weight, grad_rows, (((1,), (1,)), ((), ())), preferred_element_type=F32)
    bbuf[c] = back.astype(BF16)

    for o in range(1, NZ):
        send(bbuf.at[c], bbuf.at[c], b_send.at[0, o - 1], b_recv.at[c], coldev((z + o) % NZ, x))
    for d in range(1, NX):
        send(bbuf.at[c], bbuf.at[c], b_send.at[d, 0], b_recv.at[c], coldev(z, (x + d) % NX))
    act_ref[...] = (summed * sigma).astype(BF16)
    wown[...] = jnp.dot(aggregated.astype(F32).T.astype(BF16), grad_rows, preferred_element_type=F32)
    wx = wown.shape[0] // NX
    wyn = wx // NY
    m = [0]

    def wsend(src, dst, slot, device):
        send(src, dst, w_send.at[m[0]], w_recv.at[slot], device)
        m[0] += 1

    for d in range(1, NX):
        wsend(wown.at[pl.ds(((x + d) % NX) * wx, wx)], rw1.at[d - 1], d - 1, coldev(z, (x + d) % NX))
    for o in range(1, NZ):
        t = ((z + NZ - o) % NZ) * NX + x
        arrived(bbuf.at[t], b_recv.at[t])
        for d in range(1, NX):
            send(bbuf.at[t], bbuf.at[t], b_send.at[d, o], b_recv.at[t], coldev(z, (x + d) % NX))
    total = wown[pl.ds(x * wx, wx), :]
    for d in range(1, NX):
        arrived(rw1.at[d - 1], w_recv.at[d - 1])
        total += rw1[d - 1]
    ws2[...] = total
    base = NX - 1
    for d in range(1, NY):
        wsend(ws2.at[pl.ds(((y + d) % NY) * wyn, wyn)], rw2.at[d - 1], base + d - 1, rowdev((y + d) % NY, h, core))
    for o in range(NZ):
        for d in range(1, NX):
            t = ((z + NZ - o) % NZ) * NX + (x + d) % NX
            arrived(bbuf.at[t], b_recv.at[t])
    total = ws2[pl.ds(y * wyn, wyn), :]
    for d in range(1, NY):
        arrived(rw2.at[d - 1], w_recv.at[base + d - 1])
        total += rw2[d - 1]
    base += NY - 1
    ws3[...] = total
    wsend(ws3, rw3, base, rowdev(y, h, 1 - core))

    product_scan(4, lambda i, s: jnp.dot(bbuf[s], vals[i], preferred_element_type=F32))

    for o in range(1, NY + 1):
        yy = (y + o) % NY
        for cc in range(NC):
            for hh in range(NH):
                qpack[cc, yy, hh] = sums[tabs[7, tile_of(yy, hh, cc)]]
        send(
            qpack.at[1 - core, yy], rq.at[yy], qc_send.at[o - 1], qc_recv.at[yy], rowdev(y, h, 1 - core)
        )
    arrived(rw3, w_recv.at[base])
    total = ws3[...] + rw3[...]
    ws4[...] = total
    base += 1
    for o in range(1, NZ):
        wsend(ws4, rw4.at[o - 1], base + o - 1, coldev((z + o) % NZ, x))
    for o in range(1, NY + 1):
        yy = (y + o) % NY
        arrived(rq.at[yy], qc_recv.at[yy])
        pair = qpack[core, yy].astype(F32) + rq[yy].astype(F32)
        if o < NY:
            ys[o - 1] = pair.astype(BF16)
            send(ys.at[o - 1], ry.at[o - 1], qy_send.at[o - 1], qy_recv.at[o - 1], rowdev(yy, h, core))
        else:
            ys[o - 1] = pair.astype(BF16)
    for o in range(1, NZ):
        arrived(rw4.at[o - 1], w_recv.at[base + o - 1])
        total += rw4[o - 1]
    base += NZ - 1
    ws5[...] = total
    wsend(ws5, rw5, base, rowdev(y, 1 - h, core))
    for o in range(1, NY):
        arrived(ry.at[o - 1], qy_recv.at[o - 1])
    away = ys[NY - 1, 1 - h].astype(F32)
    mine = ys[NY - 1, h].astype(F32)
    for o in range(1, NY):
        away += ry[o - 1, 1 - h].astype(F32)
    zh[...] = away.astype(BF16)
    send(zh, rzh, qh_send, qh_recv, rowdev(y, 1 - h, core))
    for o in range(1, NY):
        mine += ry[o - 1, h].astype(F32)
    arrived(rw5, w_recv.at[base])
    base += 1
    wy[pl.ds(y * wyn, wyn), :] = (ws5[...] + rw5[...]) * scale
    piece = wy.at[pl.ds(y * wyn, wyn)]
    for d in range(1, NY):
        wsend(piece, piece, base + d - 1, rowdev((y + d) % NY, h, core))
    for d in range(1, NY):
        arrived(wy.at[pl.ds(((y + NY - d) % NY) * wyn, wyn)], w_recv.at[base + d - 1])
    base += NY - 1
    wall[pl.ds(x * wx, wx), :] = wy[...]
    piece = wall.at[pl.ds(x * wx, wx)]
    for d in range(1, NX):
        wsend(piece, piece, base + d - 1, coldev(z, (x + d) % NX))
    arrived(rzh, qh_recv)
    fg_ref[...] = (mine + rzh[...].astype(F32)).T.astype(BF16)
    for d in range(1, NX):
        arrived(wall.at[pl.ds(((x + NX - d) % NX) * wx, wx)], w_recv.at[base + d - 1])
    wg_ref[...] = wall[...]
    for copy in sent:
        copy.wait_send()


def per_device(features, weight, tile_values, tile_row, tile_col, tile_count, upstream):
    rows, width = features.shape
    hidden = weight.shape[1]
    slots = tile_values.shape[1]
    nodes = rows * lax.axis_size("row") * lax.axis_size("col")
    tile = (T, T)
    wx = width // NX
    wyn = wx // NY
    dma = pltpu.SemaphoreType.DMA
    vm = pl.BlockSpec(memory_space=pltpu.VMEM)
    w_count = (NX - 1) + (NY - 1) + 1 + (NZ - 1) + 1 + (NY - 1) + (NX - 1)
    flops = 2 * 2 * slots * T * T * T
    return pl.pallas_call(
        functools.partial(kernel, 1.0 / math.sqrt(nodes)),
        out_shape=(
            jax.ShapeDtypeStruct((rows, hidden), BF16),
            jax.ShapeDtypeStruct((rows, width), BF16),
            jax.ShapeDtypeStruct((width, hidden), F32),
        ),
        in_specs=[
            vm, vm, pl.BlockSpec(memory_space=pl.ANY), vm, vm, pl.BlockSpec(memory_space=pltpu.SMEM), vm,
        ],
        out_specs=(vm, vm, vm),
        scratch_shapes=[
            pltpu.VMEM((slots,) + tile, BF16),
            pltpu.VMEM((NY * NH * NC,) + tile, BF16),
            pltpu.VMEM((slots + 1,) + tile, BF16),
            pltpu.VMEM((NX, NZ) + tile, BF16),
            pltpu.VMEM((NX - 1, NZ) + tile, BF16),
            pltpu.VMEM((NZ - 1,) + tile, BF16),
            pltpu.VMEM((NZ - 1,) + tile, BF16),
            pltpu.VMEM((NZ * NX,) + tile, BF16),
            pltpu.VMEM((NC, NY, NH) + tile, BF16),
            pltpu.VMEM((NY, NH) + tile, BF16),
            pltpu.VMEM((NY, NH) + tile, BF16),
            pltpu.VMEM((max(NY - 1, 1), NH) + tile, BF16),
            pltpu.VMEM(tile, BF16),
            pltpu.VMEM(tile, BF16),
            pltpu.VMEM((width, hidden), F32),
            pltpu.VMEM((NX - 1, wx, hidden), F32),
            pltpu.VMEM((wx, hidden), F32),
            pltpu.VMEM((max(NY - 1, 1), wyn, hidden), F32),
            pltpu.VMEM((wyn, hidden), F32),
            pltpu.VMEM((wyn, hidden), F32),
            pltpu.VMEM((wyn, hidden), F32),
            pltpu.VMEM((NZ - 1, wyn, hidden), F32),
            pltpu.VMEM((wyn, hidden), F32),
            pltpu.VMEM((wyn, hidden), F32),
            pltpu.VMEM((wx, hidden), F32),
            pltpu.VMEM((width, hidden), F32),
            pltpu.VMEM((8, slots), jnp.int32),
            pltpu.SMEM((8, slots), jnp.int32),
            dma((2,)),
            dma((NY * NH * NC,)), dma((NY * NH * NC,)),
            dma((NX - 1, NZ)), dma((NX - 1, NZ)),
            dma((NZ - 1,)), dma((NZ - 1,)),
            dma((NX, NZ)), dma((NZ * NX,)),
            dma((NY,)), dma((NY,)),
            dma((max(NY - 1, 1),)), dma((max(NY - 1, 1),)),
            dma, dma,
            dma((w_count,)), dma((w_count,)),
        ],
        compiler_params=pltpu.CompilerParams(
            collective_id=0, has_side_effects=True, vmem_limit_bytes=40 * 1024 * 1024
        ),
        cost_estimate=pl.CostEstimate(flops=flops, bytes_accessed=slots * T * T * 2, transcendentals=rows * hidden),
    )(features, weight, tile_values, tile_row, tile_col, tile_count, upstream)


def solution(mesh):
    in_specs = (
        P(("col", "row"), None),
        P(),
        P("row", "col", None, None),
        P("row", "col"),
        P("row", "col"),
        P("row", "col"),
        P(("row", "col"), None),
    )
    out_specs = (P(("row", "col"), None), P(("col", "row"), None), P())
    return jax.shard_map(
        per_device, mesh=mesh, in_specs=in_specs, out_specs=out_specs, check_vma=False
    )
```

```python
import functools
import math

import jax
import jax.numpy as jnp
from jax import lax
from jax.experimental import pallas as pl
from jax.experimental.pallas import tpu as pltpu
from jax.sharding import PartitionSpec as P

MESH = pl.DeviceIdType.MESH
F32 = jnp.float32
BF16 = jnp.bfloat16
T = 128

NX, NZ, NY, NH, NC = 4, 8, 4, 2, 2


def order_tables(target, source, live, bins):
    slots = target.shape[1]
    lane = lax.broadcasted_iota(jnp.int32, (slots, slots), 1)
    sub = lax.broadcasted_iota(jnp.int32, (slots, slots), 0)
    wide = jnp.where(lane < live, jnp.broadcast_to(target, (slots, slots)), bins)
    key = wide * slots + lane
    tall = wide.T
    tall_key = tall * slots + sub
    rank = jnp.sum((tall_key < key).astype(jnp.int32), axis=0, keepdims=True)
    tall_rank = jnp.broadcast_to(rank, (slots, slots)).T
    placed = tall_rank == lane
    tall_source = jnp.broadcast_to(source, (slots, slots)).T
    perm = jnp.sum(jnp.where(placed, sub, 0), axis=0, keepdims=True)
    src = jnp.sum(jnp.where(placed, tall_source, 0), axis=0, keepdims=True)
    place = jnp.sum(jnp.where(placed, tall, 0), axis=0, keepdims=True)
    before = jnp.sum(jnp.where(tall_rank + 1 == lane, tall, 0), axis=0, keepdims=True)
    first = lax.broadcasted_iota(jnp.int32, (1, slots), 1) == 0
    keep = jnp.where((place == before) & jnp.logical_not(first), 1, 0)
    upto = jnp.sum((tall <= lane).astype(jnp.int32), axis=0, keepdims=True)
    here = jnp.sum((tall == lane).astype(jnp.int32), axis=0, keepdims=True)
    last = jnp.where(here > 0, upto - 1, slots)
    return perm, src, keep, last


def kernel(
    scale,
    feat_hbm, weight_hbm, vals_hbm, row_hbm, col_hbm, count_hbm, up_hbm,
    act_ref, fg_ref, wg_ref,
    weight_ref, row_ref, col_ref, up_ref, count_ref,
    vals, xbuf, sums, pbuf, rx, zs, rz, bbuf, qpack, rq, ys, ry, zh, rzh,
    wown, wr1, wz, wrz, wall,
    tabv, tabs,
    local_sem, x_send, x_recv, px_send, px_recv, pz_send, pz_recv, b_send, b_recv,
    qc_send, qc_recv, qy_send, qy_recv, qh_send, qh_recv,
    w1_send, w1_recv, wz_send, wz_recv, w2_send, w2_recv,
):
    r = lax.axis_index("row")
    c = lax.axis_index("col")
    y, h, core = r // (NH * NC), (r // NC) % NH, r % NC
    z, x = c // NX, c % NX
    slots = vals.shape[0]
    sent = []

    def rowdev(yy, hh, cc):
        return {"row": (yy * NH + hh) * NC + cc, "col": c}

    def coldev(zz, xx):
        return {"row": r, "col": zz * NX + xx}

    def send(src, dst, send_sem, recv_sem, device):
        copy = pltpu.make_async_remote_copy(
            src_ref=src, dst_ref=dst, send_sem=send_sem, recv_sem=recv_sem, device_id=device, device_id_type=MESH
        )
        copy.start()
        sent.append(copy)

    def arrived(dst, recv_sem):
        pltpu.make_async_remote_copy(
            src_ref=dst, dst_ref=dst, send_sem=recv_sem, recv_sem=recv_sem, device_id=rowdev(y, h, 1 - core), device_id_type=MESH
        ).wait_recv()

    group = NX * NY * NC
    ring = NH * NZ
    place = (x * NY + y) * NC + core
    spot = h * NZ + z

    def group_device(p):
        return {"row": ((p // NC) % NY * NH + h) * NC + p % NC, "col": z * NX + p // (NY * NC)}

    def ring_device(p):
        return {"row": (y * NH + p // NZ) * NC + core, "col": (p % NZ) * NX + x}

    barrier = pltpu.get_barrier_semaphore()

    def greet_ring(g, carry):
        pl.semaphore_signal(barrier, inc=1, device_id=ring_device((spot + g) % ring), device_id_type=MESH)
        return carry

    def greet_group(g, carry):
        pl.semaphore_signal(barrier, inc=1, device_id=group_device((place + g) % group), device_id_type=MESH)
        return carry

    pl.semaphore_signal(barrier, inc=1, device_id=rowdev(y, 1 - h, core), device_id_type=MESH)
    lax.fori_loop(1, ring // 2, greet_ring, 0)
    lax.fori_loop(ring // 2 + 1, ring, greet_ring, 0)
    lax.fori_loop(1, group, greet_group, 0)
    own_copies = [
        pltpu.make_async_copy(src, dst, local_sem.at[i])
        for i, (src, dst) in enumerate([
            (row_hbm, row_ref), (col_hbm, col_ref), (count_hbm, count_ref), (feat_hbm, xbuf.at[r]),
            (weight_hbm, weight_ref), (up_hbm, up_ref), (vals_hbm.at[0], vals),
        ])
    ]
    for copy in own_copies:
        copy.start()
    pl.semaphore_wait(barrier, ring + group - 2)

    def tile_of(yy, hh, cc):
        return (yy * NH + hh) * NC + cc

    n = [0]

    def share(tile, device):
        send(xbuf.at[tile], xbuf.at[tile], x_send.at[n[0]], x_recv.at[tile], device)
        n[0] += 1

    def share_own(device):
        send(feat_hbm, xbuf.at[r], x_send.at[n[0]], x_recv.at[r], device)
        n[0] += 1

    share_own(rowdev(y, 1 - h, core))
    for d in range(1, NY):
        share_own(rowdev((y + d) % NY, h, core))
    share_own(rowdev(y, h, 1 - core))
    for copy in own_copies[:3]:
        copy.wait()
    live = count_ref[0, 0]
    forward = order_tables(row_ref[...], col_ref[...], live, NZ * NX)
    for i, table in enumerate(forward):
        tabv[i : i + 1, :] = table
    backward = order_tables(col_ref[...], row_ref[...], live, NY * NH * NC)
    for i, table in enumerate(backward):
        tabv[4 + i : 5 + i, :] = table
    tabs_copy = pltpu.make_async_copy(tabv, tabs, local_sem.at[7])
    tabs_copy.start()
    sums[slots] = jnp.zeros((T, T), BF16)
    def pass_on(hh):
        for d in (1, 3, 2):
            tile = tile_of((y + d) % NY, hh, core)
            arrived(xbuf.at[tile], x_recv.at[tile])
            share(tile, rowdev(y, h, 1 - core))

    pass_on(h)
    other = tile_of(y, 1 - h, core)
    arrived(xbuf.at[other], x_recv.at[other])
    for d in range(1, NY):
        share(other, rowdev((y + d) % NY, h, core))
    share(other, rowdev(y, h, 1 - core))
    pass_on(1 - h)
    for hh in range(NH):
        for yy in range(NY):
            tile = tile_of(yy, hh, 1 - core)
            arrived(xbuf.at[tile], x_recv.at[tile])

    tabs_copy.wait()
    for copy in own_copies[3:]:
        copy.wait()

    def product_scan(base, multiply):
        def body(step, total):
            for u in range(8):
                k = step * 8 + u
                keep = tabs[base + 2, k].astype(F32)
                total = total * keep + multiply(tabs[base, k], tabs[base + 1, k])
                sums[k] = total.astype(BF16)
            return total

        lax.fori_loop(0, slots // 8, body, jnp.zeros((T, T), F32))

    product_scan(0, lambda i, s: jnp.dot(vals[i], xbuf[s], preferred_element_type=F32))

    def near(k):
        side = jnp.minimum(z, NZ - 1 - z)
        both = k <= 2 * side
        far = jnp.where(both, (k + 1) // 2, k - side)
        up = jnp.where(both, k % 2 == 1, z < NZ // 2)
        return z + jnp.where(up, far, -far)

    order = [near(k) for k in range(NZ - 1, 0, -1)] + [z]
    for zz in order:
        for xx in range(NX):
            pbuf[xx, zz] = sums[tabs[3, zz * NX + xx]]
        for d in range(1, NX):
            send(
                pbuf.at[(x + d) % NX, zz], rx.at[d - 1, zz],
                px_send.at[d - 1, zz], px_recv.at[d - 1, zz], coldev(z, (x + d) % NX),
            )
    for o, zz in enumerate(order):
        total = pbuf[x, zz].astype(F32)
        for d in range(1, NX):
            arrived(rx.at[d - 1, zz], px_recv.at[d - 1, zz])
            total += rx[d - 1, zz].astype(F32)
        if o < NZ - 1:
            zs[zz] = total.astype(BF16)
            send(zs.at[zz], rz.at[z], pz_send.at[zz], pz_recv.at[z], coldev(zz, x))
    for zz in order[:-1]:
        arrived(rz.at[zz], pz_recv.at[zz])
        total += rz[zz].astype(F32)
    aggregated = total.astype(BF16)

    weight = weight_ref[...]
    summed = jnp.dot(aggregated, weight, preferred_element_type=F32)
    sigma = jax.nn.sigmoid(summed)
    slope = sigma * (1.0 + summed * (1.0 - sigma))
    grad_rows = (up_ref[...].astype(F32) * slope).astype(BF16)
    back = lax.dot_general(weight, grad_rows, (((1,), (1,)), ((), ())), preferred_element_type=F32)
    bbuf[c] = back.astype(BF16)

    side = z + 1 - 2 * (z % 2)
    turn = 2 - 4 * (z // 2 % 2)
    mates = [side, z + turn, side + turn]
    across = (z + NZ // 2) % NZ
    for zz in [across] + mates:
        send(bbuf.at[c], bbuf.at[c], b_send.at[0, zz], b_recv.at[c], coldev(zz, x))
    for d in range(1, NX):
        send(bbuf.at[c], bbuf.at[c], b_send.at[d, z], b_recv.at[c], coldev(z, (x + d) % NX))
    act_ref[...] = (summed * sigma).astype(BF16)
    term = jnp.dot(aggregated.astype(F32).T.astype(BF16), grad_rows, preferred_element_type=F32)
    high, wide = wown.shape[1:]
    blocks = [(i * high, j * wide) for i in range(term.shape[0] // high) for j in range(term.shape[1] // wide)]
    for i, (top, left) in enumerate(blocks):
        wown[i] = term[top : top + high, left : left + wide]
    def give_pieces(g, carry):
        p = (place + g) % group
        pltpu.make_async_remote_copy(
            src_ref=wown.at[p], dst_ref=wr1.at[place], send_sem=w1_send.at[p], recv_sem=w1_recv.at[place],
            device_id=group_device(p), device_id_type=MESH,
        ).start()
        return carry

    lax.fori_loop(1, group, give_pieces, 0)
    for i, zz in enumerate([side, across] + mates[1:] + [(mate + NZ // 2) % NZ for mate in mates]):
        t = zz * NX + x
        arrived(bbuf.at[t], b_recv.at[t])
        if i == 1:
            for mate in mates:
                send(bbuf.at[t], bbuf.at[t], b_send.at[0, (mate + NZ // 2) % NZ], b_recv.at[t], coldev(mate, x))
        for d in range(1, NX):
            send(bbuf.at[t], bbuf.at[t], b_send.at[d, zz], b_recv.at[t], coldev(z, (x + d) % NX))

    def take_pieces(g, total):
        p = (place + g) % group
        arrived(wr1.at[p], w1_recv.at[p])
        return total + wr1[p]

    piece = lax.fori_loop(1, group, take_pieces, wown[place])
    wz[...] = piece

    def give_ring(g, carry):
        p = (spot + g) % ring
        pltpu.make_async_remote_copy(
            src_ref=wz, dst_ref=wrz.at[spot], send_sem=wz_send.at[p], recv_sem=wz_recv.at[spot],
            device_id=ring_device(p), device_id_type=MESH,
        ).start()
        return carry

    lax.fori_loop(1, ring, give_ring, 0)
    for k in range(NZ):
        for d in range(1, NX):
            t = (near(k) if k else z) * NX + (x + d) % NX
            arrived(bbuf.at[t], b_recv.at[t])

    product_scan(4, lambda i, s: jnp.dot(bbuf[s], vals[i], preferred_element_type=F32))

    for o in range(1, NY + 1):
        yy = (y + o) % NY
        for cc in range(NC):
            for hh in range(NH):
                qpack[cc, yy, hh] = sums[tabs[7, tile_of(yy, hh, cc)]]
        send(
            qpack.at[1 - core, yy], rq.at[yy], qc_send.at[o - 1], qc_recv.at[yy], rowdev(y, h, 1 - core)
        )
    for o in range(1, NY + 1):
        yy = (y + o) % NY
        arrived(rq.at[yy], qc_recv.at[yy])
        pair = qpack[core, yy].astype(F32) + rq[yy].astype(F32)
        if o < NY:
            ys[o - 1] = pair.astype(BF16)
            send(ys.at[o - 1], ry.at[o - 1], qy_send.at[o - 1], qy_recv.at[o - 1], rowdev(yy, h, core))
        else:
            ys[o - 1] = pair.astype(BF16)
    for o in range(1, NY):
        arrived(ry.at[o - 1], qy_recv.at[o - 1])
    away = ys[NY - 1, 1 - h].astype(F32)
    mine = ys[NY - 1, h].astype(F32)
    for o in range(1, NY):
        away += ry[o - 1, 1 - h].astype(F32)
    zh[...] = away.astype(BF16)
    send(zh, rzh, qh_send, qh_recv, rowdev(y, 1 - h, core))
    for o in range(1, NY):
        mine += ry[o - 1, h].astype(F32)
    def take_ring(g, total):
        p = (spot + g) % ring
        arrived(wrz.at[p], wz_recv.at[p])
        return total + wrz[p]

    wall[place] = lax.fori_loop(1, ring, take_ring, piece) * scale

    def give_sums(g, carry):
        p = (place + g) % group
        pltpu.make_async_remote_copy(
            src_ref=wall.at[place], dst_ref=wall.at[place], send_sem=w2_send.at[p], recv_sem=w2_recv.at[place],
            device_id=group_device(p), device_id_type=MESH,
        ).start()
        return carry

    lax.fori_loop(1, group, give_sums, 0)

    def take_sums(g, carry):
        p = (place + g) % group
        arrived(wall.at[p], w2_recv.at[p])
        return carry

    lax.fori_loop(1, group, take_sums, 0)
    for i, (top, left) in enumerate(blocks):
        wg_ref[top : top + high, left : left + wide] = wall[i]
    arrived(rzh, qh_recv)
    fg_ref[...] = (mine + rzh[...].astype(F32)).T.astype(BF16)
    for copy in sent:
        copy.wait_send()

    def sent_group(g, carry):
        p = (place + g) % group
        for src, sem in ((wown.at[p], w1_send.at[p]), (wall.at[place], w2_send.at[p])):
            pltpu.make_async_remote_copy(
                src_ref=src, dst_ref=src, send_sem=sem, recv_sem=sem,
                device_id=group_device(p), device_id_type=MESH,
            ).wait_send()
        return carry

    def sent_ring(g, carry):
        p = (spot + g) % ring
        pltpu.make_async_remote_copy(
            src_ref=wz, dst_ref=wz, send_sem=wz_send.at[p], recv_sem=wz_send.at[p],
            device_id=ring_device(p), device_id_type=MESH,
        ).wait_send()
        return carry

    lax.fori_loop(1, group, sent_group, 0)
    lax.fori_loop(1, ring, sent_ring, 0)


def per_device(features, weight, tile_values, tile_row, tile_col, tile_count, upstream):
    rows, width = features.shape
    hidden = weight.shape[1]
    slots = tile_values.shape[1]
    nodes = rows * lax.axis_size("row") * lax.axis_size("col")
    tile = (T, T)
    group = NX * NY * NC
    ring = NH * NZ
    piece = (8, 128)
    dma = pltpu.SemaphoreType.DMA
    vm = pl.BlockSpec(memory_space=pltpu.VMEM)
    hbm = pl.BlockSpec(memory_space=pl.ANY)
    flops = 2 * 2 * slots * T * T * T
    return pl.pallas_call(
        functools.partial(kernel, 1.0 / math.sqrt(nodes)),
        out_shape=(
            pltpu.VMEM((rows, hidden), BF16),
            pltpu.VMEM((rows, width), BF16),
            pltpu.VMEM((width, hidden), F32),
        ),
        in_specs=[hbm] * 7,
        out_specs=(vm, vm, vm),
        scratch_shapes=[
            pltpu.VMEM(weight.shape, BF16),
            pltpu.VMEM(tile_row.shape, jnp.int32),
            pltpu.VMEM(tile_col.shape, jnp.int32),
            pltpu.VMEM(upstream.shape, BF16),
            pltpu.SMEM(tile_count.shape, jnp.int32),
            pltpu.VMEM((slots,) + tile, BF16),
            pltpu.VMEM((NY * NH * NC,) + tile, BF16),
            pltpu.VMEM((slots + 1,) + tile, BF16),
            pltpu.VMEM((NX, NZ) + tile, BF16),
            pltpu.VMEM((NX - 1, NZ) + tile, BF16),
            pltpu.VMEM((NZ,) + tile, BF16),
            pltpu.VMEM((NZ,) + tile, BF16),
            pltpu.VMEM((NZ * NX,) + tile, BF16),
            pltpu.VMEM((NC, NY, NH) + tile, BF16),
            pltpu.VMEM((NY, NH) + tile, BF16),
            pltpu.VMEM((NY, NH) + tile, BF16),
            pltpu.VMEM((max(NY - 1, 1), NH) + tile, BF16),
            pltpu.VMEM(tile, BF16),
            pltpu.VMEM(tile, BF16),
            pltpu.VMEM((group,) + piece, F32),
            pltpu.VMEM((group,) + piece, F32),
            pltpu.VMEM(piece, F32),
            pltpu.VMEM((ring,) + piece, F32),
            pltpu.VMEM((group,) + piece, F32),
            pltpu.VMEM((8, slots), jnp.int32),
            pltpu.SMEM((8, slots), jnp.int32),
            dma((8,)),
            dma((NY * NH * NC,)), dma((NY * NH * NC,)),
            dma((NX - 1, NZ)), dma((NX - 1, NZ)),
            dma((NZ,)), dma((NZ,)),
            dma((NX, NZ)), dma((NZ * NX,)),
            dma((NY,)), dma((NY,)),
            dma((max(NY - 1, 1),)), dma((max(NY - 1, 1),)),
            dma, dma,
            dma((group,)), dma((group,)),
            dma((ring,)), dma((ring,)),
            dma((group,)), dma((group,)),
        ],
        compiler_params=pltpu.CompilerParams(
            collective_id=0, has_side_effects=True, vmem_limit_bytes=56 * 1024 * 1024
        ),
        cost_estimate=pl.CostEstimate(flops=flops, bytes_accessed=slots * T * T * 2, transcendentals=rows * hidden),
    )(features, weight, tile_values, tile_row, tile_col, tile_count, upstream)


def solution(mesh):
    in_specs = (
        P(("col", "row"), None),
        P(),
        P("row", "col", None, None),
        P("row", "col"),
        P("row", "col"),
        P("row", "col"),
        P(("row", "col"), None),
    )
    out_specs = (P(("row", "col"), None), P(("col", "row"), None), P())
    return jax.shard_map(
        per_device, mesh=mesh, in_specs=in_specs, out_specs=out_specs, check_vma=False
    )
```

```python
import functools
import math

import jax
import jax.numpy as jnp
from jax import lax
from jax.experimental import pallas as pl
from jax.experimental.pallas import tpu as pltpu
from jax.sharding import PartitionSpec as P

MESH = pl.DeviceIdType.MESH
F32 = jnp.float32
BF16 = jnp.bfloat16
T = 128

NX, NZ, NY, NH, NC = 4, 8, 4, 2, 2
UNROLL = 64


def order_tables(target, source, live, bins):
    slots = target.shape[1]
    lane = lax.broadcasted_iota(jnp.int32, (slots, slots), 1)
    sub = lax.broadcasted_iota(jnp.int32, (slots, slots), 0)
    wide = jnp.where(lane < live, jnp.broadcast_to(target, (slots, slots)), bins)
    key = wide * slots + lane
    tall = wide.T
    tall_key = tall * slots + sub
    rank = jnp.sum((tall_key < key).astype(jnp.int32), axis=0, keepdims=True)
    tall_rank = jnp.broadcast_to(rank, (slots, slots)).T
    placed = tall_rank == lane
    tall_source = jnp.broadcast_to(source, (slots, slots)).T
    perm = jnp.sum(jnp.where(placed, sub, 0), axis=0, keepdims=True)
    src = jnp.sum(jnp.where(placed, tall_source, 0), axis=0, keepdims=True)
    place = jnp.sum(jnp.where(placed, tall, 0), axis=0, keepdims=True)
    before = jnp.sum(jnp.where(tall_rank + 1 == lane, tall, 0), axis=0, keepdims=True)
    first = lax.broadcasted_iota(jnp.int32, (1, slots), 1) == 0
    keep = jnp.where((place == before) & jnp.logical_not(first), 1, 0)
    upto = jnp.sum((tall <= lane).astype(jnp.int32), axis=0, keepdims=True)
    here = jnp.sum((tall == lane).astype(jnp.int32), axis=0, keepdims=True)
    last = jnp.where(here > 0, upto - 1, slots)
    return perm, src, keep, last


def kernel(
    scale,
    feat_hbm, weight_hbm, vals_hbm, row_hbm, col_hbm, count_hbm, up_hbm,
    act_ref, fg_ref, wg_ref,
    weight_ref, row_ref, col_ref, up_ref, count_ref,
    vals, xbuf, sums, pbuf, rx, zs, rz, bbuf, qpack, rq, ys, ry, zh, rzh,
    wown, wr1, wz, wrz, wall,
    tabv, tabs,
    local_sem, x_send, xh_recv, xy_recv, xk_recv, px_send, px_recv, pz_send, pz_recv,
    b_send, bz_recv, bx_recv, q_send, qk_recv, qy_recv, qh_recv,
    w_send, w_recv,
):
    r = lax.axis_index("row")
    c = lax.axis_index("col")
    core, h, y = lax.rem(r, NC), lax.rem(lax.div(r, NC), NH), lax.div(r, NC * NH)
    x, z = lax.rem(c, NX), lax.div(c, NX)
    slots = vals.shape[0]
    on_x = [lax.rem(x + d, NX) for d in range(NX)]
    on_y = [lax.rem(y + d, NY) for d in range(NY)]
    on_h = [h, 1 - h]
    on_core = [core, 1 - core]

    def tile_of(yy, hh, cc):
        return (yy * NH + hh) * NC + cc

    def rowdev(yy, hh, cc):
        return {"row": tile_of(yy, hh, cc), "col": c}

    def coldev(zz, xx):
        return {"row": r, "col": zz * NX + xx}

    group = [(dx, dy, dc) for dx in range(NX) for dy in range(NY) for dc in range(NC)]
    ring = NH * NZ
    spot = h * NZ + z

    def piece_of(xx, yy, cc):
        return (xx * NY + yy) * NC + cc

    def group_device(dx, dy, dc):
        return {"row": tile_of(on_y[dy], h, on_core[dc]), "col": z * NX + on_x[dx]}

    def ring_device(g):
        p = lax.rem(spot + g, ring)
        hh = lax.div(p, NZ)
        return {"row": tile_of(y, hh, core), "col": (p - hh * NZ) * NX + x}

    def send(src, dst, send_sem, recv_sem, device):
        pltpu.make_async_remote_copy(
            src_ref=src, dst_ref=dst, send_sem=send_sem, recv_sem=recv_sem, device_id=device, device_id_type=MESH
        ).start()

    def waiter(ref, sem):
        return pltpu.make_async_remote_copy(
            src_ref=ref, dst_ref=ref, send_sem=sem, recv_sem=sem,
            device_id=rowdev(y, h, on_core[1]), device_id_type=MESH,
        )

    def arrived(ref, sem):
        waiter(ref, sem).wait_recv()

    barrier = pltpu.get_barrier_semaphore()
    peers = [ring_device(g) for g in [ring // 2] + [g for g in range(1, ring) if g != ring // 2]]
    peers += [group_device(*g) for g in group[1:]]
    for peer in peers:
        pl.semaphore_signal(barrier, inc=1, device_id=peer, device_id_type=MESH)
    own_copies = [
        pltpu.make_async_copy(src, dst, local_sem.at[i])
        for i, (src, dst) in enumerate([
            (row_hbm, row_ref), (col_hbm, col_ref), (count_hbm, count_ref), (feat_hbm, xbuf.at[r]),
            (weight_hbm, weight_ref), (up_hbm, up_ref), (vals_hbm.at[0], vals),
        ])
    ]
    for copy in own_copies:
        copy.start()
    pl.semaphore_wait(barrier, len(peers))

    def share(tile, recv_sem, device, src=None):
        send(xbuf.at[tile] if src is None else src, xbuf.at[tile], x_send, recv_sem, device)

    share(r, xh_recv, rowdev(y, on_h[1], core), feat_hbm)
    for d in range(1, NY):
        share(r, xy_recv.at[0, d - 1], rowdev(on_y[d], h, core), feat_hbm)
    share(r, xk_recv, rowdev(y, h, on_core[1]), feat_hbm)
    for copy in own_copies[:3]:
        copy.wait()
    live = count_ref[0, 0]
    forward = order_tables(row_ref[...], col_ref[...], live, NZ * NX)
    for i, table in enumerate(forward):
        tabv[i : i + 1, :] = table
    backward = order_tables(col_ref[...], row_ref[...], live, NY * NH * NC)
    for i, table in enumerate(backward):
        tabv[4 + i : 5 + i, :] = table
    tabs_copy = pltpu.make_async_copy(tabv, tabs, local_sem.at[7])
    tabs_copy.start()
    sums[slots] = jnp.zeros((T, T), BF16)

    for i in range(NH):
        if i == 1:
            other = tile_of(y, on_h[1], core)
            arrived(xbuf.at[other], xh_recv)
            for d in range(1, NY):
                share(other, xy_recv.at[1, d - 1], rowdev(on_y[d], h, core))
            share(other, xk_recv, rowdev(y, h, on_core[1]))
        for d in (1, 3, 2):
            tile = tile_of(on_y[d], on_h[i], core)
            arrived(xbuf.at[tile], xy_recv.at[i, NY - d - 1])
            share(tile, xk_recv, rowdev(y, h, on_core[1]))
    arrived(xbuf.at[pl.ds(0, NY * NH)], xk_recv)

    tabs_copy.wait()
    for copy in own_copies[3:]:
        copy.wait()

    def product_scan(base, multiply):
        def body(step, total):
            for u in range(UNROLL):
                k = step * UNROLL + u
                keep = tabs[base + 2, k].astype(F32)
                total = total * keep + multiply(tabs[base, k], tabs[base + 1, k])
                sums[k] = total.astype(BF16)
            return total

        lax.fori_loop(0, slots // UNROLL, body, jnp.zeros((T, T), F32))

    product_scan(0, lambda i, s: jnp.dot(vals[i], xbuf[s], preferred_element_type=F32))

    def near(k):
        side = jnp.minimum(z, NZ - 1 - z)
        both = k <= 2 * side
        far = jnp.where(both, (k + 1) // 2, k - side)
        up = jnp.where(both, k % 2 == 1, z < NZ // 2)
        return z + jnp.where(up, far, -far)

    order = [near(k) for k in range(NZ - 1, 0, -1)] + [z]
    for zz in order:
        for xx in range(NX):
            pbuf[xx, zz] = sums[tabs[3, zz * NX + xx]]
        for d in (1, 3, 2):
            send(pbuf.at[on_x[d], zz], rx.at[zz, d - 1], px_send, px_recv.at[zz], coldev(z, on_x[d]))
    for o, zz in enumerate(order):
        arrived(rx.at[zz], px_recv.at[zz])
        total = pbuf[x, zz].astype(F32)
        for d in range(1, NX):
            total += rx[zz, d - 1].astype(F32)
        if o < NZ - 1:
            zs[zz] = total.astype(BF16)
            slot = lax.rem(zz - z + NZ, NZ) - 1
            send(zs.at[zz], rz.at[slot], pz_send, pz_recv, coldev(zz, x))
    arrived(rz, pz_recv)
    for o in range(NZ - 1):
        total += rz[o].astype(F32)
    aggregated = total.astype(BF16)

    weight = weight_ref[...]
    summed = jnp.dot(aggregated, weight, preferred_element_type=F32)
    sigma = jax.nn.sigmoid(summed)
    slope = sigma * (1.0 + summed * (1.0 - sigma))
    grad_rows = (up_ref[...].astype(F32) * slope).astype(BF16)
    back = lax.dot_general(weight, grad_rows, (((1,), (1,)), ((), ())), preferred_element_type=F32)
    bbuf[c] = back.astype(BF16)

    side = z + 1 - 2 * lax.rem(z, 2)
    turn = 2 - 4 * lax.rem(lax.div(z, 2), 2)
    mates = [side, z + turn, side + turn]
    across = lax.rem(z + NZ // 2, NZ)
    far = [lax.rem(mate + NZ // 2, NZ) for mate in mates]

    def give_back(t, recv_sem, device):
        send(bbuf.at[t], bbuf.at[t], b_send, recv_sem, device)

    give_back(c, bz_recv.at[0], coldev(across, x))
    for i, mate in enumerate(mates):
        give_back(c, bz_recv.at[1 + i], coldev(mate, x))
    for d in (1, 3, 2):
        give_back(c, bx_recv, coldev(z, on_x[d]))
    act_ref[...] = (summed * sigma).astype(BF16)
    term = jnp.dot(aggregated.astype(F32).T.astype(BF16), grad_rows, preferred_element_type=F32)
    high, wide = wown.shape[1:]
    blocks = [(i * high, j * wide) for i in range(term.shape[0] // high) for j in range(term.shape[1] // wide)]
    for i, (top, left) in enumerate(blocks):
        wown[i] = term[top : top + high, left : left + wide]
    for g, (dx, dy, dc) in enumerate(group[1:]):
        send(
            wown.at[piece_of(on_x[dx], on_y[dy], on_core[dc])], wr1.at[g], w_send.at[0], w_recv.at[0],
            group_device(dx, dy, dc),
        )
    for zz, sem in [(side, 1), (across, 0), (mates[1], 2), (mates[2], 3), (far[0], 4), (far[1], 5), (far[2], 6)]:
        t = zz * NX + x
        arrived(bbuf.at[t], bz_recv.at[sem])
        if sem == 0:
            for i, mate in enumerate(mates):
                give_back(t, bz_recv.at[4 + i], coldev(mate, x))
        for d in (1, 3, 2):
            give_back(t, bx_recv, coldev(z, on_x[d]))

    place = piece_of(x, y, core)
    arrived(wr1, w_recv.at[0])
    piece = wown[place]
    for g in range(len(group) - 1):
        piece += wr1[g]
    wz[...] = piece
    for g in [ring // 2] + [g for g in range(1, ring) if g != ring // 2]:
        send(wz, wrz.at[g - 1], w_send.at[1], w_recv.at[1], ring_device(g))
    arrived(bbuf.at[pl.ds(0, (NX - 1) * NZ)], bx_recv)

    product_scan(4, lambda i, s: jnp.dot(bbuf[s], vals[i], preferred_element_type=F32))

    for j in (1, 0):
        for i in (1, 0):
            for yy in range(NY):
                qpack[j, i, yy] = sums[tabs[7, tile_of(yy, on_h[i], on_core[j])]]
            if j == 1:
                send(qpack.at[j, i], rq.at[i], q_send, qk_recv.at[i], rowdev(y, h, on_core[1]))
    own = {}
    for i in (1, 0):
        arrived(rq.at[i], qk_recv.at[i])
        for d in range(1, NY):
            yy = on_y[d]
            ys[i, d - 1] = (qpack[0, i, yy].astype(F32) + rq[i, yy].astype(F32)).astype(BF16)
            send(ys.at[i, d - 1], ry.at[i, d - 1], q_send, qy_recv.at[i], rowdev(yy, h, core))
        own[i] = qpack[0, i, y].astype(F32) + rq[i, y].astype(F32)
    arrived(ry.at[1], qy_recv.at[1])
    for d in range(NY - 1):
        own[1] += ry[1, d].astype(F32)
    zh[...] = own[1].astype(BF16)
    send(zh, rzh, q_send, qh_recv, rowdev(y, on_h[1], core))
    arrived(wrz, w_recv.at[1])
    for g in range(ring - 1):
        piece += wrz[g]
    wall[place] = piece * scale
    for g in group[1:]:
        send(wall.at[place], wall.at[place], w_send.at[2], w_recv.at[2], group_device(*g))
    arrived(ry.at[0], qy_recv.at[0])
    for d in range(NY - 1):
        own[0] += ry[0, d].astype(F32)
    waiter(xbuf.at[pl.ds(0, NY * NH * NC - 1)], x_send).wait_send()
    waiter(rx, px_send).wait_send()
    waiter(rz, pz_send).wait_send()
    waiter(bbuf.at[pl.ds(0, NZ * NX - 1)], b_send).wait_send()
    waiter(xbuf.at[pl.ds(0, NH * NY + NH * (NY - 1) + 1)], q_send).wait_send()
    waiter(wr1, w_send.at[0]).wait_send()
    waiter(wrz, w_send.at[1]).wait_send()
    waiter(wr1, w_send.at[2]).wait_send()
    arrived(wr1, w_recv.at[2])
    for i, (top, left) in enumerate(blocks):
        wg_ref[top : top + high, left : left + wide] = wall[i]
    arrived(rzh, qh_recv)
    fg_ref[...] = (own[0] + rzh[...].astype(F32)).T.astype(BF16)


def per_device(features, weight, tile_values, tile_row, tile_col, tile_count, upstream):
    rows, width = features.shape
    hidden = weight.shape[1]
    slots = tile_values.shape[1]
    nodes = rows * lax.axis_size("row") * lax.axis_size("col")
    tile = (T, T)
    group = NX * NY * NC
    ring = NH * NZ
    piece = (8, 128)
    dma = pltpu.SemaphoreType.DMA
    vm = pl.BlockSpec(memory_space=pltpu.VMEM)
    hbm = pl.BlockSpec(memory_space=pl.ANY)
    flops = 2 * 2 * slots * T * T * T
    return pl.pallas_call(
        functools.partial(kernel, 1.0 / math.sqrt(nodes)),
        out_shape=(
            pltpu.VMEM((rows, hidden), BF16),
            pltpu.VMEM((rows, width), BF16),
            pltpu.VMEM((width, hidden), F32),
        ),
        in_specs=[hbm] * 7,
        out_specs=(vm, vm, vm),
        scratch_shapes=[
            pltpu.VMEM(weight.shape, BF16),
            pltpu.VMEM(tile_row.shape, jnp.int32),
            pltpu.VMEM(tile_col.shape, jnp.int32),
            pltpu.VMEM(upstream.shape, BF16),
            pltpu.SMEM(tile_count.shape, jnp.int32),
            pltpu.VMEM((slots,) + tile, BF16),
            pltpu.VMEM((NY * NH * NC,) + tile, BF16),
            pltpu.VMEM((slots + 1,) + tile, BF16),
            pltpu.VMEM((NX, NZ) + tile, BF16),
            pltpu.VMEM((NZ, NX - 1) + tile, BF16),
            pltpu.VMEM((NZ,) + tile, BF16),
            pltpu.VMEM((NZ - 1,) + tile, BF16),
            pltpu.VMEM((NZ * NX,) + tile, BF16),
            pltpu.VMEM((NC, NH, NY) + tile, BF16),
            pltpu.VMEM((NH, NY) + tile, BF16),
            pltpu.VMEM((NH, NY - 1) + tile, BF16),
            pltpu.VMEM((NH, NY - 1) + tile, BF16),
            pltpu.VMEM(tile, BF16),
            pltpu.VMEM(tile, BF16),
            pltpu.VMEM((group,) + piece, F32),
            pltpu.VMEM((group - 1,) + piece, F32),
            pltpu.VMEM(piece, F32),
            pltpu.VMEM((ring - 1,) + piece, F32),
            pltpu.VMEM((group,) + piece, F32),
            pltpu.VMEM((8, slots), jnp.int32),
            pltpu.SMEM((8, slots), jnp.int32),
            dma((8,)),
            dma, dma, dma((NH, NY - 1)), dma,
            dma, dma((NZ,)), dma, dma,
            dma, dma((NZ - 1,)), dma,
            dma, dma((NH,)), dma((NH,)), dma,
            dma((3,)), dma((3,)),
        ],
        compiler_params=pltpu.CompilerParams(
            collective_id=0, has_side_effects=True, vmem_limit_bytes=56 * 1024 * 1024
        ),
        cost_estimate=pl.CostEstimate(flops=flops, bytes_accessed=slots * T * T * 2, transcendentals=rows * hidden),
    )(features, weight, tile_values, tile_row, tile_col, tile_count, upstream)


def solution(mesh):
    in_specs = (
        P(("col", "row"), None),
        P(),
        P("row", "col", None, None),
        P("row", "col"),
        P("row", "col"),
        P("row", "col"),
        P(("row", "col"), None),
    )
    out_specs = (P(("row", "col"), None), P(("col", "row"), None), P())
    return jax.shard_map(
        per_device, mesh=mesh, in_specs=in_specs, out_specs=out_specs, check_vma=False
    )
```

```python
import functools
import math

import jax
import jax.numpy as jnp
from jax import lax
from jax.experimental import pallas as pl
from jax.experimental.pallas import tpu as pltpu
from jax.sharding import PartitionSpec as P

MESH = pl.DeviceIdType.MESH
F32 = jnp.float32
BF16 = jnp.bfloat16
T = 128

NX, NZ, NY, NH, NC = 4, 8, 4, 2, 2
UNROLL = 64


def order_tables(target, source, live, bins):
    slots = target.shape[1]
    lane = lax.broadcasted_iota(jnp.int32, (slots, slots), 1)
    sub = lax.broadcasted_iota(jnp.int32, (slots, slots), 0)
    wide = jnp.where(lane < live, jnp.broadcast_to(target, (slots, slots)), bins)
    key = wide * slots + lane
    tall = wide.T
    tall_key = tall * slots + sub
    rank = jnp.sum((tall_key < key).astype(jnp.int32), axis=0, keepdims=True)
    tall_rank = jnp.broadcast_to(rank, (slots, slots)).T
    placed = tall_rank == lane
    tall_source = jnp.broadcast_to(source, (slots, slots)).T
    perm = jnp.sum(jnp.where(placed, sub, 0), axis=0, keepdims=True)
    src = jnp.sum(jnp.where(placed, tall_source, 0), axis=0, keepdims=True)
    place = jnp.sum(jnp.where(placed, tall, 0), axis=0, keepdims=True)
    before = jnp.sum(jnp.where(tall_rank + 1 == lane, tall, 0), axis=0, keepdims=True)
    first = lax.broadcasted_iota(jnp.int32, (1, slots), 1) == 0
    keep = jnp.where((place == before) & jnp.logical_not(first), 1, 0)
    upto = jnp.sum((tall <= lane).astype(jnp.int32), axis=0, keepdims=True)
    here = jnp.sum((tall == lane).astype(jnp.int32), axis=0, keepdims=True)
    last = jnp.where(here > 0, upto - 1, slots)
    return perm, src, keep, last


def kernel(
    scale,
    feat_hbm, weight_hbm, vals_hbm, row_hbm, col_hbm, count_hbm, up_hbm,
    act_ref, fg_ref, wg_ref,
    weight_ref, row_ref, col_ref, up_ref, count_ref,
    vals, xbuf, sums, pbuf, rx, zs, rz, bbuf, qpack, rq, ys, ry, zh, rzh,
    wown, wr1, wz, wrz, wall,
    tabv, tabs,
    local_sem, x_send, xh_recv, xy_recv, xk_recv, px_send, px_recv, pz_send, pz_recv,
    b_send, bz_recv, bx_recv, q_send, qk_recv, qy_recv, qh_recv,
    w_send, w_recv,
):
    r = lax.axis_index("row")
    c = lax.axis_index("col")
    core, h, y = lax.rem(r, NC), lax.rem(lax.div(r, NC), NH), lax.div(r, NC * NH)
    x, z = lax.rem(c, NX), lax.div(c, NX)
    slots = vals.shape[0]
    on_x = [lax.rem(x + d, NX) for d in range(NX)]
    on_y = [lax.rem(y + d, NY) for d in range(NY)]
    on_h = [h, 1 - h]
    on_core = [core, 1 - core]

    def tile_of(yy, hh, cc):
        return (yy * NH + hh) * NC + cc

    def rowdev(yy, hh, cc):
        return {"row": tile_of(yy, hh, cc), "col": c}

    def coldev(zz, xx):
        return {"row": r, "col": zz * NX + xx}

    group = [(dx, dy, dc) for dx in range(NX) for dy in range(NY) for dc in range(NC)]
    ring = NH * NZ
    spot = h * NZ + z

    def piece_of(xx, yy, cc):
        return (xx * NY + yy) * NC + cc

    def group_device(dx, dy, dc):
        return {"row": tile_of(on_y[dy], h, on_core[dc]), "col": z * NX + on_x[dx]}

    def ring_device(g):
        p = lax.rem(spot + g, ring)
        hh = lax.div(p, NZ)
        return {"row": tile_of(y, hh, core), "col": (p - hh * NZ) * NX + x}

    def send(src, dst, send_sem, recv_sem, device):
        pltpu.make_async_remote_copy(
            src_ref=src, dst_ref=dst, send_sem=send_sem, recv_sem=recv_sem, device_id=device, device_id_type=MESH
        ).start()

    def waiter(ref, sem):
        return pltpu.make_async_remote_copy(
            src_ref=ref, dst_ref=ref, send_sem=sem, recv_sem=sem,
            device_id=rowdev(y, h, on_core[1]), device_id_type=MESH,
        )

    def arrived(ref, sem):
        waiter(ref, sem).wait_recv()

    barrier = pltpu.get_barrier_semaphore()
    peers = [ring_device(g) for g in [ring // 2] + [g for g in range(1, ring) if g != ring // 2]]
    peers += [group_device(*g) for g in group[1:]]
    for peer in peers:
        pl.semaphore_signal(barrier, inc=1, device_id=peer, device_id_type=MESH)
    own_copies = [
        pltpu.make_async_copy(src, dst, local_sem.at[i])
        for i, (src, dst) in enumerate([
            (row_hbm, row_ref), (col_hbm, col_ref), (count_hbm, count_ref), (feat_hbm, xbuf.at[r]),
            (weight_hbm, weight_ref), (up_hbm, up_ref), (vals_hbm.at[0], vals),
        ])
    ]
    for copy in own_copies:
        copy.start()
    own_copies[3].wait()
    pl.semaphore_wait(barrier, len(peers))

    def share(tile, recv_sem, device):
        send(xbuf.at[tile], xbuf.at[tile], x_send, recv_sem, device)

    share(r, xh_recv, rowdev(y, on_h[1], core))
    for d in range(1, NY):
        share(r, xy_recv.at[0, d - 1], rowdev(on_y[d], h, core))
    share(r, xk_recv, rowdev(y, h, on_core[1]))
    for copy in own_copies[:3]:
        copy.wait()
    live = count_ref[0, 0]
    forward = order_tables(row_ref[...], col_ref[...], live, NZ * NX)
    for i, table in enumerate(forward):
        tabv[i : i + 1, :] = table
    backward = order_tables(col_ref[...], row_ref[...], live, NY * NH * NC)
    for i, table in enumerate(backward):
        tabv[4 + i : 5 + i, :] = table
    tabs_copy = pltpu.make_async_copy(tabv, tabs, local_sem.at[7])
    tabs_copy.start()
    sums[slots] = jnp.zeros((T, T), BF16)

    for i in range(NH):
        if i == 1:
            other = tile_of(y, on_h[1], core)
            arrived(xbuf.at[other], xh_recv)
            for d in range(1, NY):
                share(other, xy_recv.at[1, d - 1], rowdev(on_y[d], h, core))
            share(other, xk_recv, rowdev(y, h, on_core[1]))
        for d in (1, 3, 2):
            tile = tile_of(on_y[d], on_h[i], core)
            arrived(xbuf.at[tile], xy_recv.at[i, NY - d - 1])
            share(tile, xk_recv, rowdev(y, h, on_core[1]))
    arrived(xbuf.at[pl.ds(0, NY * NH)], xk_recv)

    tabs_copy.wait()
    for copy in own_copies[4:]:
        copy.wait()

    def product_scan(base, multiply):
        def body(step, total):
            for u in range(UNROLL):
                k = step * UNROLL + u
                keep = tabs[base + 2, k].astype(F32)
                total = total * keep + multiply(tabs[base, k], tabs[base + 1, k])
                sums[k] = total.astype(BF16)
            return total

        lax.fori_loop(0, slots // UNROLL, body, jnp.zeros((T, T), F32))

    product_scan(0, lambda i, s: jnp.dot(vals[i], xbuf[s], preferred_element_type=F32))

    def near(k):
        side = jnp.minimum(z, NZ - 1 - z)
        both = k <= 2 * side
        far = jnp.where(both, (k + 1) // 2, k - side)
        up = jnp.where(both, k % 2 == 1, z < NZ // 2)
        return z + jnp.where(up, far, -far)

    order = [near(k) for k in range(NZ - 1, 0, -1)] + [z]
    for zz in order:
        for xx in range(NX):
            pbuf[xx, zz] = sums[tabs[3, zz * NX + xx]]
        for d in (1, 3, 2):
            send(pbuf.at[on_x[d], zz], rx.at[zz, d - 1], px_send, px_recv.at[zz], coldev(z, on_x[d]))
    for o, zz in enumerate(order):
        arrived(rx.at[zz], px_recv.at[zz])
        total = pbuf[x, zz].astype(F32)
        for d in range(1, NX):
            total += rx[zz, d - 1].astype(F32)
        if o < NZ - 1:
            zs[zz] = total.astype(BF16)
            slot = lax.rem(zz - z + NZ, NZ) - 1
            send(zs.at[zz], rz.at[slot], pz_send, pz_recv, coldev(zz, x))
    arrived(rz, pz_recv)
    for o in range(NZ - 1):
        total += rz[o].astype(F32)
    aggregated = total.astype(BF16)

    weight = weight_ref[...]
    summed = jnp.dot(aggregated, weight, preferred_element_type=F32)
    sigma = jax.nn.sigmoid(summed)
    slope = sigma * (1.0 + summed * (1.0 - sigma))
    grad_rows = (up_ref[...].astype(F32) * slope).astype(BF16)
    back = lax.dot_general(weight, grad_rows, (((1,), (1,)), ((), ())), preferred_element_type=F32)
    bbuf[c] = back.astype(BF16)

    side = z + 1 - 2 * lax.rem(z, 2)
    turn = 2 - 4 * lax.rem(lax.div(z, 2), 2)
    mates = [side, z + turn, side + turn]
    across = lax.rem(z + NZ // 2, NZ)
    far = [lax.rem(mate + NZ // 2, NZ) for mate in mates]

    def give_back(t, recv_sem, device):
        send(bbuf.at[t], bbuf.at[t], b_send, recv_sem, device)

    give_back(c, bz_recv.at[0], coldev(across, x))
    for i, mate in enumerate(mates):
        give_back(c, bz_recv.at[1 + i], coldev(mate, x))
    for d in (1, 3, 2):
        give_back(c, bx_recv, coldev(z, on_x[d]))
    act_ref[...] = (summed * sigma).astype(BF16)
    term = jnp.dot(aggregated.astype(F32).T.astype(BF16), grad_rows, preferred_element_type=F32)
    high, wide = wown.shape[1:]
    blocks = [(i * high, j * wide) for i in range(term.shape[0] // high) for j in range(term.shape[1] // wide)]
    for i, (top, left) in enumerate(blocks):
        wown[i] = term[top : top + high, left : left + wide]
    for g, (dx, dy, dc) in enumerate(group[1:]):
        send(
            wown.at[piece_of(on_x[dx], on_y[dy], on_core[dc])], wr1.at[g], w_send.at[0], w_recv.at[0],
            group_device(dx, dy, dc),
        )
    last = NZ - 1
    for zz, sem in [(side, 1), (across, 0), (mates[1], 2), (mates[2], 3), (across, last), (far[0], 4), (far[1], 5), (far[2], 6)]:
        t = zz * NX + (on_x[2] if sem == last else x)
        arrived(bbuf.at[t], bz_recv.at[sem])
        if sem in (0, last):
            for i, mate in enumerate(mates):
                give_back(t, bx_recv if sem == last else bz_recv.at[4 + i], coldev(mate, x))
        if sem != last:
            for d in (1, 3, 2)[: 2 if sem >= 4 else 3]:
                give_back(t, bz_recv.at[last] if (sem, d) == (0, 2) else bx_recv, coldev(z, on_x[d]))

    place = piece_of(x, y, core)
    arrived(wr1, w_recv.at[0])
    piece = wown[place]
    for g in range(len(group) - 1):
        piece += wr1[g]
    wz[...] = piece
    for g in [ring // 2] + [g for g in range(1, ring) if g != ring // 2]:
        send(wz, wrz.at[g - 1], w_send.at[1], w_recv.at[1], ring_device(g))
    arrived(bbuf.at[pl.ds(0, (NX - 1) * NZ - 1)], bx_recv)

    product_scan(4, lambda i, s: jnp.dot(bbuf[s], vals[i], preferred_element_type=F32))

    for j in (1, 0):
        for i in (1, 0):
            for yy in range(NY):
                qpack[j, i, yy] = sums[tabs[7, tile_of(yy, on_h[i], on_core[j])]]
            if j == 1:
                send(qpack.at[j, i], rq.at[i], q_send, qk_recv.at[i], rowdev(y, h, on_core[1]))
    own = {}
    for i in (1, 0):
        arrived(rq.at[i], qk_recv.at[i])
        for d in range(1, NY):
            yy = on_y[d]
            ys[i, d - 1] = (qpack[0, i, yy].astype(F32) + rq[i, yy].astype(F32)).astype(BF16)
            send(ys.at[i, d - 1], ry.at[i, d - 1], q_send, qy_recv.at[i], rowdev(yy, h, core))
        own[i] = qpack[0, i, y].astype(F32) + rq[i, y].astype(F32)
    arrived(ry.at[1], qy_recv.at[1])
    for d in range(NY - 1):
        own[1] += ry[1, d].astype(F32)
    zh[...] = own[1].astype(BF16)
    send(zh, rzh, q_send, qh_recv, rowdev(y, on_h[1], core))
    arrived(wrz, w_recv.at[1])
    for g in range(ring - 1):
        piece += wrz[g]
    wall[place] = piece * scale
    for g in group[1:]:
        send(wall.at[place], wall.at[place], w_send.at[2], w_recv.at[2], group_device(*g))
    arrived(ry.at[0], qy_recv.at[0])
    for d in range(NY - 1):
        own[0] += ry[0, d].astype(F32)
    waiter(xbuf.at[pl.ds(0, NY * NH * NC - 1)], x_send).wait_send()
    waiter(rx, px_send).wait_send()
    waiter(rz, pz_send).wait_send()
    waiter(bbuf.at[pl.ds(0, NZ * NX - 1)], b_send).wait_send()
    waiter(xbuf.at[pl.ds(0, NH * NY + NH * (NY - 1) + 1)], q_send).wait_send()
    waiter(wr1, w_send.at[0]).wait_send()
    waiter(wrz, w_send.at[1]).wait_send()
    waiter(wr1, w_send.at[2]).wait_send()
    arrived(wr1, w_recv.at[2])
    for i, (top, left) in enumerate(blocks):
        wg_ref[top : top + high, left : left + wide] = wall[i]
    arrived(rzh, qh_recv)
    fg_ref[...] = (own[0] + rzh[...].astype(F32)).T.astype(BF16)


def per_device(features, weight, tile_values, tile_row, tile_col, tile_count, upstream):
    rows, width = features.shape
    hidden = weight.shape[1]
    slots = tile_values.shape[1]
    nodes = rows * lax.axis_size("row") * lax.axis_size("col")
    tile = (T, T)
    group = NX * NY * NC
    ring = NH * NZ
    piece = (8, 128)
    dma = pltpu.SemaphoreType.DMA
    vm = pl.BlockSpec(memory_space=pltpu.VMEM)
    hbm = pl.BlockSpec(memory_space=pl.ANY)
    flops = 2 * 2 * slots * T * T * T
    return pl.pallas_call(
        functools.partial(kernel, 1.0 / math.sqrt(nodes)),
        out_shape=(
            pltpu.VMEM((rows, hidden), BF16),
            pltpu.VMEM((rows, width), BF16),
            pltpu.VMEM((width, hidden), F32),
        ),
        in_specs=[hbm] * 7,
        out_specs=(vm, vm, vm),
        scratch_shapes=[
            pltpu.VMEM(weight.shape, BF16),
            pltpu.VMEM(tile_row.shape, jnp.int32),
            pltpu.VMEM(tile_col.shape, jnp.int32),
            pltpu.VMEM(upstream.shape, BF16),
            pltpu.SMEM(tile_count.shape, jnp.int32),
            pltpu.VMEM((slots,) + tile, BF16),
            pltpu.VMEM((NY * NH * NC,) + tile, BF16),
            pltpu.VMEM((slots + 1,) + tile, BF16),
            pltpu.VMEM((NX, NZ) + tile, BF16),
            pltpu.VMEM((NZ, NX - 1) + tile, BF16),
            pltpu.VMEM((NZ,) + tile, BF16),
            pltpu.VMEM((NZ - 1,) + tile, BF16),
            pltpu.VMEM((NZ * NX,) + tile, BF16),
            pltpu.VMEM((NC, NH, NY) + tile, BF16),
            pltpu.VMEM((NH, NY) + tile, BF16),
            pltpu.VMEM((NH, NY - 1) + tile, BF16),
            pltpu.VMEM((NH, NY - 1) + tile, BF16),
            pltpu.VMEM(tile, BF16),
            pltpu.VMEM(tile, BF16),
            pltpu.VMEM((group,) + piece, F32),
            pltpu.VMEM((group - 1,) + piece, F32),
            pltpu.VMEM(piece, F32),
            pltpu.VMEM((ring - 1,) + piece, F32),
            pltpu.VMEM((group,) + piece, F32),
            pltpu.VMEM((8, slots), jnp.int32),
            pltpu.SMEM((8, slots), jnp.int32),
            dma((8,)),
            dma, dma, dma((NH, NY - 1)), dma,
            dma, dma((NZ,)), dma, dma,
            dma, dma((NZ,)), dma,
            dma, dma((NH,)), dma((NH,)), dma,
            dma((3,)), dma((3,)),
        ],
        compiler_params=pltpu.CompilerParams(
            collective_id=0, has_side_effects=True, vmem_limit_bytes=56 * 1024 * 1024
        ),
        cost_estimate=pl.CostEstimate(flops=flops, bytes_accessed=slots * T * T * 2, transcendentals=rows * hidden),
    )(features, weight, tile_values, tile_row, tile_col, tile_count, upstream)


def solution(mesh):
    in_specs = (
        P(("col", "row"), None),
        P(),
        P("row", "col", None, None),
        P("row", "col"),
        P("row", "col"),
        P("row", "col"),
        P(("row", "col"), None),
    )
    out_specs = (P(("row", "col"), None), P(("col", "row"), None), P())
    return jax.shard_map(
        per_device, mesh=mesh, in_specs=in_specs, out_specs=out_specs, check_vma=False
    )
```

```python
import functools
import math

import jax
import jax.numpy as jnp
from jax import lax
from jax.experimental import pallas as pl
from jax.experimental.pallas import tpu as pltpu
from jax.sharding import PartitionSpec as P

MESH = pl.DeviceIdType.MESH
F32 = jnp.float32
BF16 = jnp.bfloat16
T = 128

NX, NZ, NY, NH, NC = 4, 8, 4, 2, 2
UNROLL = 64


def order_tables(target, source, live, bins):
    slots = target.shape[1]
    lane = lax.broadcasted_iota(jnp.int32, (slots, slots), 1)
    sub = lax.broadcasted_iota(jnp.int32, (slots, slots), 0)
    wide = jnp.where(lane < live, jnp.broadcast_to(target, (slots, slots)), bins)
    key = wide * slots + lane
    tall = wide.T
    tall_key = tall * slots + sub
    rank = jnp.sum((tall_key < key).astype(jnp.int32), axis=0, keepdims=True)
    tall_rank = jnp.broadcast_to(rank, (slots, slots)).T
    placed = tall_rank == lane
    tall_source = jnp.broadcast_to(source, (slots, slots)).T
    perm = jnp.sum(jnp.where(placed, sub, 0), axis=0, keepdims=True)
    src = jnp.sum(jnp.where(placed, tall_source, 0), axis=0, keepdims=True)
    place = jnp.sum(jnp.where(placed, tall, 0), axis=0, keepdims=True)
    before = jnp.sum(jnp.where(tall_rank + 1 == lane, tall, 0), axis=0, keepdims=True)
    first = lax.broadcasted_iota(jnp.int32, (1, slots), 1) == 0
    keep = jnp.where((place == before) & jnp.logical_not(first), 1, 0)
    upto = jnp.sum((tall <= lane).astype(jnp.int32), axis=0, keepdims=True)
    here = jnp.sum((tall == lane).astype(jnp.int32), axis=0, keepdims=True)
    last = jnp.where(here > 0, upto - 1, slots)
    return perm, src, keep, last


def kernel(
    scale,
    feat_hbm, weight_hbm, vals_hbm, row_hbm, col_hbm, count_hbm, up_hbm,
    act_ref, fg_ref, wg_ref,
    weight_ref, row_ref, col_ref, up_ref, count_ref,
    vals, xbuf, sums, pbuf, rx, zs, rz, bbuf, qpack, rq, ys, ry, zh, rzh,
    wown, wr1, wz, wrz, wall,
    tabv, tabs,
    local_sem, x_send, xh_recv, xy_recv, xk_recv, px_send, px_recv, pz_send, pz_recv,
    b_send, bz_recv, bx_recv, q_send, qk_recv, qy_recv, qh_recv,
    w_send, w_recv,
):
    r = lax.axis_index("row")
    c = lax.axis_index("col")
    core, h, y = lax.rem(r, NC), lax.rem(lax.div(r, NC), NH), lax.div(r, NC * NH)
    x, z = lax.rem(c, NX), lax.div(c, NX)
    slots = vals.shape[0]
    on_x = [lax.rem(x + d, NX) for d in range(NX)]
    on_y = [lax.rem(y + d, NY) for d in range(NY)]
    on_h = [h, 1 - h]
    on_core = [core, 1 - core]

    def tile_of(yy, hh, cc):
        return (yy * NH + hh) * NC + cc

    def rowdev(yy, hh, cc):
        return {"row": tile_of(yy, hh, cc), "col": c}

    def coldev(zz, xx):
        return {"row": r, "col": zz * NX + xx}

    group = [(dx, dy, dc) for dx in range(NX) for dy in range(NY) for dc in range(NC)]
    ring = NH * NZ
    spot = h * NZ + z

    def piece_of(xx, yy, cc):
        return (xx * NY + yy) * NC + cc

    def group_device(dx, dy, dc):
        return {"row": tile_of(on_y[dy], h, on_core[dc]), "col": z * NX + on_x[dx]}

    def ring_device(g):
        p = lax.rem(spot + g, ring)
        hh = lax.div(p, NZ)
        return {"row": tile_of(y, hh, core), "col": (p - hh * NZ) * NX + x}

    def send(src, dst, send_sem, recv_sem, device):
        pltpu.make_async_remote_copy(
            src_ref=src, dst_ref=dst, send_sem=send_sem, recv_sem=recv_sem, device_id=device, device_id_type=MESH
        ).start()

    def waiter(ref, sem):
        return pltpu.make_async_remote_copy(
            src_ref=ref, dst_ref=ref, send_sem=sem, recv_sem=sem,
            device_id=rowdev(y, h, on_core[1]), device_id_type=MESH,
        )

    def arrived(ref, sem):
        waiter(ref, sem).wait_recv()

    barrier = pltpu.get_barrier_semaphore()
    peers = [ring_device(g) for g in [ring // 2] + [g for g in range(1, ring) if g != ring // 2]]
    peers += [group_device(*g) for g in group[1:]]
    for peer in peers:
        pl.semaphore_signal(barrier, inc=1, device_id=peer, device_id_type=MESH)
    own_copies = [
        pltpu.make_async_copy(src, dst, local_sem.at[i])
        for i, (src, dst) in enumerate([
            (row_hbm, row_ref), (col_hbm, col_ref), (count_hbm, count_ref), (feat_hbm, xbuf.at[r]),
            (weight_hbm, weight_ref), (up_hbm, up_ref), (vals_hbm.at[0], vals),
        ])
    ]
    for copy in own_copies:
        copy.start()
    own_copies[3].wait()
    pl.semaphore_wait(barrier, len(peers))

    def share(tile, recv_sem, device):
        send(xbuf.at[tile], xbuf.at[tile], x_send, recv_sem, device)

    share(r, xh_recv, rowdev(y, on_h[1], core))
    for d in range(1, NY):
        share(r, xy_recv.at[0, d - 1], rowdev(on_y[d], h, core))
    share(r, xk_recv, rowdev(y, h, on_core[1]))
    for copy in own_copies[:3]:
        copy.wait()
    live = count_ref[0, 0]
    forward = order_tables(row_ref[...], col_ref[...], live, NZ * NX)
    for i, table in enumerate(forward):
        tabv[i : i + 1, :] = table
    backward = order_tables(col_ref[...], row_ref[...], live, NY * NH * NC)
    for i, table in enumerate(backward):
        tabv[4 + i : 5 + i, :] = table
    tabs_copy = pltpu.make_async_copy(tabv, tabs, local_sem.at[7])
    tabs_copy.start()
    sums[slots] = jnp.zeros((T, T), BF16)

    for i in range(NH):
        if i == 1:
            other = tile_of(y, on_h[1], core)
            arrived(xbuf.at[other], xh_recv)
            for d in range(1, NY):
                share(other, xy_recv.at[1, d - 1], rowdev(on_y[d], h, core))
            share(other, xk_recv, rowdev(y, h, on_core[1]))
        for d in (1, 3, 2):
            tile = tile_of(on_y[d], on_h[i], core)
            arrived(xbuf.at[tile], xy_recv.at[i, NY - d - 1])
            share(tile, xk_recv, rowdev(y, h, on_core[1]))
    arrived(xbuf.at[pl.ds(0, NY * NH)], xk_recv)

    tabs_copy.wait()
    for copy in own_copies[4:]:
        copy.wait()

    def product_scan(base, multiply):
        def body(step, total):
            for u in range(UNROLL):
                k = step * UNROLL + u
                keep = tabs[base + 2, k].astype(F32)
                total = total * keep + multiply(tabs[base, k], tabs[base + 1, k])
                sums[k] = total.astype(BF16)
            return total

        lax.fori_loop(0, slots // UNROLL, body, jnp.zeros((T, T), F32))

    product_scan(0, lambda i, s: jnp.dot(vals[i], xbuf[s], preferred_element_type=F32))

    def near(k):
        side = jnp.minimum(z, NZ - 1 - z)
        both = k <= 2 * side
        far = jnp.where(both, (k + 1) // 2, k - side)
        up = jnp.where(both, k % 2 == 1, z < NZ // 2)
        return z + jnp.where(up, far, -far)

    order = [near(k) for k in range(NZ - 1, 0, -1)] + [z]
    for zz in order:
        for xx in range(NX):
            pbuf[xx, zz] = sums[tabs[3, zz * NX + xx]]
        for d in (1, 3, 2):
            send(pbuf.at[on_x[d], zz], rx.at[zz, d - 1], px_send, px_recv.at[zz], coldev(z, on_x[d]))
    for o, zz in enumerate(order):
        arrived(rx.at[zz], px_recv.at[zz])
        total = pbuf[x, zz].astype(F32)
        for d in range(1, NX):
            total += rx[zz, d - 1].astype(F32)
        if o < NZ - 1:
            zs[zz] = total.astype(BF16)
            slot = lax.rem(zz - z + NZ, NZ) - 1
            send(zs.at[zz], rz.at[slot], pz_send, pz_recv, coldev(zz, x))
    arrived(rz, pz_recv)
    for o in range(NZ - 1):
        total += rz[o].astype(F32)
    aggregated = total.astype(BF16)

    weight = weight_ref[...]
    summed = jnp.dot(aggregated, weight, preferred_element_type=F32)
    sigma = jax.nn.sigmoid(summed)
    slope = sigma * (1.0 + summed * (1.0 - sigma))
    grad_rows = (up_ref[...].astype(F32) * slope).astype(BF16)
    back = lax.dot_general(weight, grad_rows, (((1,), (1,)), ((), ())), preferred_element_type=F32)
    bbuf[c] = back.astype(BF16)

    side = z + 1 - 2 * lax.rem(z, 2)
    turn = 2 - 4 * lax.rem(lax.div(z, 2), 2)
    mates = [side, z + turn, side + turn]
    across = lax.rem(z + NZ // 2, NZ)
    far = [lax.rem(mate + NZ // 2, NZ) for mate in mates]

    def give_back(t, recv_sem, device):
        send(bbuf.at[t], bbuf.at[t], b_send, recv_sem, device)

    give_back(c, bz_recv.at[0], coldev(across, x))
    for i, mate in enumerate(mates):
        give_back(c, bz_recv.at[1 + i], coldev(mate, x))
    for d in (1, 3, 2):
        give_back(c, bx_recv, coldev(z, on_x[d]))
    act_ref[...] = (summed * sigma).astype(BF16)
    term = jnp.dot(aggregated.astype(F32).T.astype(BF16), grad_rows, preferred_element_type=F32)
    high, wide = wown.shape[1:]
    blocks = [(i * high, j * wide) for i in range(term.shape[0] // high) for j in range(term.shape[1] // wide)]
    for i, (top, left) in enumerate(blocks):
        wown[i] = term[top : top + high, left : left + wide]
    for g, (dx, dy, dc) in enumerate(group[1:]):
        send(
            wown.at[piece_of(on_x[dx], on_y[dy], on_core[dc])], wr1.at[g], w_send.at[0], w_recv.at[0],
            group_device(dx, dy, dc),
        )
    last = NZ - 1
    for zz, sem in [(side, 1), (across, 0), (mates[1], 2), (mates[2], 3), (across, last), (far[0], 4), (far[1], 5), (far[2], 6)]:
        t = zz * NX + (on_x[2] if sem == last else x)
        arrived(bbuf.at[t], bz_recv.at[sem])
        if sem in (0, last):
            for i, mate in reversed(list(enumerate(mates))):
                give_back(t, bx_recv if sem == last else bz_recv.at[4 + i], coldev(mate, x))
        if sem != last:
            for d in (1, 3, 2)[: 2 if sem >= 4 else 3]:
                give_back(t, bz_recv.at[last] if (sem, d) == (0, 2) else bx_recv, coldev(z, on_x[d]))

    place = piece_of(x, y, core)
    arrived(wr1, w_recv.at[0])
    piece = wown[place]
    for g in range(len(group) - 1):
        piece += wr1[g]
    wz[...] = piece
    for g in [ring // 2] + [g for g in range(1, ring) if g != ring // 2]:
        send(wz, wrz.at[g - 1], w_send.at[1], w_recv.at[1], ring_device(g))
    arrived(bbuf.at[pl.ds(0, (NX - 1) * NZ - 1)], bx_recv)

    product_scan(4, lambda i, s: jnp.dot(bbuf[s], vals[i], preferred_element_type=F32))

    for j in (1, 0):
        for i in (1, 0):
            for yy in range(NY):
                qpack[j, i, yy] = sums[tabs[7, tile_of(yy, on_h[i], on_core[j])]]
            if j == 1:
                send(qpack.at[j, i], rq.at[i], q_send, qk_recv.at[i], rowdev(y, h, on_core[1]))
    own = {}
    for i in (1, 0):
        arrived(rq.at[i], qk_recv.at[i])
        for d in range(1, NY):
            yy = on_y[d]
            ys[i, d - 1] = (qpack[0, i, yy].astype(F32) + rq[i, yy].astype(F32)).astype(BF16)
            send(ys.at[i, d - 1], ry.at[i, d - 1], q_send, qy_recv.at[i], rowdev(yy, h, core))
        own[i] = qpack[0, i, y].astype(F32) + rq[i, y].astype(F32)
    arrived(ry.at[1], qy_recv.at[1])
    for d in range(NY - 1):
        own[1] += ry[1, d].astype(F32)
    zh[...] = own[1].astype(BF16)
    send(zh, rzh, q_send, qh_recv, rowdev(y, on_h[1], core))
    arrived(wrz, w_recv.at[1])
    for g in range(ring - 1):
        piece += wrz[g]
    wall[place] = piece * scale
    for g in group[1:]:
        send(wall.at[place], wall.at[place], w_send.at[2], w_recv.at[2], group_device(*g))
    arrived(ry.at[0], qy_recv.at[0])
    for d in range(NY - 1):
        own[0] += ry[0, d].astype(F32)
    waiter(xbuf.at[pl.ds(0, NY * NH * NC - 1)], x_send).wait_send()
    waiter(rx, px_send).wait_send()
    waiter(rz, pz_send).wait_send()
    waiter(bbuf.at[pl.ds(0, NZ * NX - 1)], b_send).wait_send()
    waiter(xbuf.at[pl.ds(0, NH * NY + NH * (NY - 1) + 1)], q_send).wait_send()
    waiter(wr1, w_send.at[0]).wait_send()
    waiter(wrz, w_send.at[1]).wait_send()
    waiter(wr1, w_send.at[2]).wait_send()
    arrived(wr1, w_recv.at[2])
    for i, (top, left) in enumerate(blocks):
        wg_ref[top : top + high, left : left + wide] = wall[i]
    arrived(rzh, qh_recv)
    fg_ref[...] = (own[0] + rzh[...].astype(F32)).T.astype(BF16)


def per_device(features, weight, tile_values, tile_row, tile_col, tile_count, upstream):
    rows, width = features.shape
    hidden = weight.shape[1]
    slots = tile_values.shape[1]
    nodes = rows * lax.axis_size("row") * lax.axis_size("col")
    tile = (T, T)
    group = NX * NY * NC
    ring = NH * NZ
    piece = (8, 128)
    dma = pltpu.SemaphoreType.DMA
    vm = pl.BlockSpec(memory_space=pltpu.VMEM)
    hbm = pl.BlockSpec(memory_space=pl.ANY)
    flops = 2 * 2 * slots * T * T * T
    return pl.pallas_call(
        functools.partial(kernel, 1.0 / math.sqrt(nodes)),
        out_shape=(
            pltpu.VMEM((rows, hidden), BF16),
            pltpu.VMEM((rows, width), BF16),
            pltpu.VMEM((width, hidden), F32),
        ),
        in_specs=[hbm] * 7,
        out_specs=(vm, vm, vm),
        scratch_shapes=[
            pltpu.VMEM(weight.shape, BF16),
            pltpu.VMEM(tile_row.shape, jnp.int32),
            pltpu.VMEM(tile_col.shape, jnp.int32),
            pltpu.VMEM(upstream.shape, BF16),
            pltpu.SMEM(tile_count.shape, jnp.int32),
            pltpu.VMEM((slots,) + tile, BF16),
            pltpu.VMEM((NY * NH * NC,) + tile, BF16),
            pltpu.VMEM((slots + 1,) + tile, BF16),
            pltpu.VMEM((NX, NZ) + tile, BF16),
            pltpu.VMEM((NZ, NX - 1) + tile, BF16),
            pltpu.VMEM((NZ,) + tile, BF16),
            pltpu.VMEM((NZ - 1,) + tile, BF16),
            pltpu.VMEM((NZ * NX,) + tile, BF16),
            pltpu.VMEM((NC, NH, NY) + tile, BF16),
            pltpu.VMEM((NH, NY) + tile, BF16),
            pltpu.VMEM((NH, NY - 1) + tile, BF16),
            pltpu.VMEM((NH, NY - 1) + tile, BF16),
            pltpu.VMEM(tile, BF16),
            pltpu.VMEM(tile, BF16),
            pltpu.VMEM((group,) + piece, F32),
            pltpu.VMEM((group - 1,) + piece, F32),
            pltpu.VMEM(piece, F32),
            pltpu.VMEM((ring - 1,) + piece, F32),
            pltpu.VMEM((group,) + piece, F32),
            pltpu.VMEM((8, slots), jnp.int32),
            pltpu.SMEM((8, slots), jnp.int32),
            dma((8,)),
            dma, dma, dma((NH, NY - 1)), dma,
            dma, dma((NZ,)), dma, dma,
            dma, dma((NZ,)), dma,
            dma, dma((NH,)), dma((NH,)), dma,
            dma((3,)), dma((3,)),
        ],
        compiler_params=pltpu.CompilerParams(
            collective_id=0, has_side_effects=True, vmem_limit_bytes=56 * 1024 * 1024
        ),
        cost_estimate=pl.CostEstimate(flops=flops, bytes_accessed=slots * T * T * 2, transcendentals=rows * hidden),
    )(features, weight, tile_values, tile_row, tile_col, tile_count, upstream)


def solution(mesh):
    in_specs = (
        P(("col", "row"), None),
        P(),
        P("row", "col", None, None),
        P("row", "col"),
        P("row", "col"),
        P("row", "col"),
        P(("row", "col"), None),
    )
    out_specs = (P(("row", "col"), None), P(("col", "row"), None), P())
    return jax.shard_map(
        per_device, mesh=mesh, in_specs=in_specs, out_specs=out_specs, check_vma=False
    )
```

```python
import functools
import math

import jax
import jax.numpy as jnp
from jax import lax
from jax.experimental import pallas as pl
from jax.experimental.pallas import tpu as pltpu
from jax.sharding import PartitionSpec as P

MESH = pl.DeviceIdType.MESH
F32 = jnp.float32
BF16 = jnp.bfloat16
T = 128

NX, NZ, NY, NH, NC = 4, 8, 4, 2, 2
UNROLL = 128


def order_tables(target, source, live, bins):
    slots = target.shape[1]
    lane = lax.broadcasted_iota(jnp.int32, (slots, slots), 1)
    sub = lax.broadcasted_iota(jnp.int32, (slots, slots), 0)
    wide = jnp.where(lane < live, jnp.broadcast_to(target, (slots, slots)), bins)
    key = wide * slots + lane
    tall = wide.T
    tall_key = tall * slots + sub
    rank = jnp.sum((tall_key < key).astype(jnp.int32), axis=0, keepdims=True)
    tall_rank = jnp.broadcast_to(rank, (slots, slots)).T
    placed = tall_rank == lane
    tall_source = jnp.broadcast_to(source, (slots, slots)).T
    perm = jnp.sum(jnp.where(placed, sub, 0), axis=0, keepdims=True)
    src = jnp.sum(jnp.where(placed, tall_source, 0), axis=0, keepdims=True)
    place = jnp.sum(jnp.where(placed, tall, 0), axis=0, keepdims=True)
    before = jnp.sum(jnp.where(tall_rank + 1 == lane, tall, 0), axis=0, keepdims=True)
    first = lax.broadcasted_iota(jnp.int32, (1, slots), 1) == 0
    keep = jnp.where((place == before) & jnp.logical_not(first), 1, 0)
    upto = jnp.sum((tall <= lane).astype(jnp.int32), axis=0, keepdims=True)
    here = jnp.sum((tall == lane).astype(jnp.int32), axis=0, keepdims=True)
    last = jnp.where(here > 0, upto - 1, slots)
    return perm, src, keep, last


def kernel(
    scale,
    feat_hbm, weight_hbm, vals_hbm, row_hbm, col_hbm, count_hbm, up_hbm,
    act_ref, fg_ref, wg_ref,
    weight_ref, row_ref, col_ref, up_ref, count_ref,
    vals, xbuf, sums, pbuf, rx, zs, rz, bbuf, qpack, rq, ys, ry, zh, rzh,
    wown, wr1, wz, wrz, wall,
    tabv, tabs,
    local_sem, x_send, xh_recv, xy_recv, xk_recv, px_send, px_recv, pz_send, pz_recv,
    b_send, bz_recv, bx_recv, q_send, qk_recv, qy_recv, qh_recv,
    w_send, w_recv,
):
    r = lax.axis_index("row")
    c = lax.axis_index("col")
    core, h, y = lax.rem(r, NC), lax.rem(lax.div(r, NC), NH), lax.div(r, NC * NH)
    x, z = lax.rem(c, NX), lax.div(c, NX)
    slots = vals.shape[0]
    on_x = [lax.rem(x + d, NX) for d in range(NX)]
    on_y = [lax.rem(y + d, NY) for d in range(NY)]
    on_h = [h, 1 - h]
    on_core = [core, 1 - core]

    def tile_of(yy, hh, cc):
        return (yy * NH + hh) * NC + cc

    def rowdev(yy, hh, cc):
        return {"row": tile_of(yy, hh, cc), "col": c}

    def coldev(zz, xx):
        return {"row": r, "col": zz * NX + xx}

    group = [(dx, dy, dc) for dx in range(NX) for dy in range(NY) for dc in range(NC)]
    ring = NH * NZ
    spot = h * NZ + z

    def piece_of(xx, yy, cc):
        return (xx * NY + yy) * NC + cc

    def group_device(dx, dy, dc):
        return {"row": tile_of(on_y[dy], h, on_core[dc]), "col": z * NX + on_x[dx]}

    def ring_device(g):
        p = lax.rem(spot + g, ring)
        hh = lax.div(p, NZ)
        return {"row": tile_of(y, hh, core), "col": (p - hh * NZ) * NX + x}

    def send(src, dst, send_sem, recv_sem, device):
        pltpu.make_async_remote_copy(
            src_ref=src, dst_ref=dst, send_sem=send_sem, recv_sem=recv_sem, device_id=device, device_id_type=MESH
        ).start()

    def waiter(ref, sem):
        return pltpu.make_async_remote_copy(
            src_ref=ref, dst_ref=ref, send_sem=sem, recv_sem=sem,
            device_id=rowdev(y, h, on_core[1]), device_id_type=MESH,
        )

    def arrived(ref, sem):
        waiter(ref, sem).wait_recv()

    barrier = pltpu.get_barrier_semaphore()
    peers = [ring_device(g) for g in [ring // 2] + [g for g in range(1, ring) if g != ring // 2]]
    peers += [group_device(*g) for g in group[1:]]
    for peer in peers:
        pl.semaphore_signal(barrier, inc=1, device_id=peer, device_id_type=MESH)
    own_copies = [
        pltpu.make_async_copy(src, dst, local_sem.at[i])
        for i, (src, dst) in enumerate([
            (row_hbm, row_ref), (col_hbm, col_ref), (count_hbm, count_ref), (feat_hbm, xbuf.at[r]),
            (weight_hbm, weight_ref), (up_hbm, up_ref), (vals_hbm.at[0], vals),
        ])
    ]
    for copy in own_copies:
        copy.start()
    own_copies[3].wait()
    pl.semaphore_wait(barrier, len(peers))

    def share(tile, recv_sem, device):
        send(xbuf.at[tile], xbuf.at[tile], x_send, recv_sem, device)

    share(r, xh_recv, rowdev(y, on_h[1], core))
    for d in range(1, NY):
        share(r, xy_recv.at[0, d - 1], rowdev(on_y[d], h, core))
    share(r, xk_recv, rowdev(y, h, on_core[1]))
    for copy in own_copies[:3]:
        copy.wait()
    live = count_ref[0, 0]
    forward = order_tables(row_ref[...], col_ref[...], live, NZ * NX)
    for i, table in enumerate(forward):
        tabv[i : i + 1, :] = table
    backward = order_tables(col_ref[...], row_ref[...], live, NY * NH * NC)
    for i, table in enumerate(backward):
        tabv[4 + i : 5 + i, :] = table
    tabs_copy = pltpu.make_async_copy(tabv, tabs, local_sem.at[7])
    tabs_copy.start()
    sums[slots] = jnp.zeros((T, T), BF16)

    for i in range(NH):
        if i == 1:
            other = tile_of(y, on_h[1], core)
            arrived(xbuf.at[other], xh_recv)
            for d in range(1, NY):
                share(other, xy_recv.at[1, d - 1], rowdev(on_y[d], h, core))
            share(other, xk_recv, rowdev(y, h, on_core[1]))
        for d in (1, 3, 2):
            tile = tile_of(on_y[d], on_h[i], core)
            arrived(xbuf.at[tile], xy_recv.at[i, NY - d - 1])
            share(tile, xk_recv, rowdev(y, h, on_core[1]))
    arrived(xbuf.at[pl.ds(0, NY * NH)], xk_recv)

    tabs_copy.wait()
    for copy in own_copies[4:]:
        copy.wait()

    def product_scan(base, multiply):
        def body(step, total):
            for u in range(UNROLL):
                k = step * UNROLL + u
                keep = tabs[base + 2, k].astype(F32)
                total = total * keep + multiply(tabs[base, k], tabs[base + 1, k])
                sums[k] = total.astype(BF16)
            return total

        lax.fori_loop(0, slots // UNROLL, body, jnp.zeros((T, T), F32))

    product_scan(0, lambda i, s: jnp.dot(vals[i], xbuf[s], preferred_element_type=F32))

    def near(k):
        side = jnp.minimum(z, NZ - 1 - z)
        both = k <= 2 * side
        far = jnp.where(both, (k + 1) // 2, k - side)
        up = jnp.where(both, k % 2 == 1, z < NZ // 2)
        return z + jnp.where(up, far, -far)

    order = [near(k) for k in range(NZ - 1, 0, -1)] + [z]
    for zz in order:
        for xx in range(NX):
            pbuf[xx, zz] = sums[tabs[3, zz * NX + xx]]
        for d in (1, 3, 2):
            send(pbuf.at[on_x[d], zz], rx.at[zz, d - 1], px_send, px_recv.at[zz], coldev(z, on_x[d]))
    for o, zz in enumerate(order):
        arrived(rx.at[zz], px_recv.at[zz])
        total = pbuf[x, zz].astype(F32)
        for d in range(1, NX):
            total += rx[zz, d - 1].astype(F32)
        if o < NZ - 1:
            zs[zz] = total.astype(BF16)
            slot = lax.rem(zz - z + NZ, NZ) - 1
            send(zs.at[zz], rz.at[slot], pz_send, pz_recv, coldev(zz, x))
    arrived(rz, pz_recv)
    for o in range(NZ - 1):
        total += rz[o].astype(F32)
    aggregated = total.astype(BF16)

    weight = weight_ref[...]
    summed = jnp.dot(aggregated, weight, preferred_element_type=F32)
    sigma = jax.nn.sigmoid(summed)
    slope = sigma * (1.0 + summed * (1.0 - sigma))
    grad_rows = (up_ref[...].astype(F32) * slope).astype(BF16)
    back = lax.dot_general(weight, grad_rows, (((1,), (1,)), ((), ())), preferred_element_type=F32)
    bbuf[c] = back.astype(BF16)

    side = z + 1 - 2 * lax.rem(z, 2)
    turn = 2 - 4 * lax.rem(lax.div(z, 2), 2)
    mates = [side, z + turn, side + turn]
    across = lax.rem(z + NZ // 2, NZ)
    far = [lax.rem(mate + NZ // 2, NZ) for mate in mates]

    def give_back(t, recv_sem, device):
        send(bbuf.at[t], bbuf.at[t], b_send, recv_sem, device)

    give_back(c, bz_recv.at[0], coldev(across, x))
    for i, mate in enumerate(mates):
        give_back(c, bz_recv.at[1 + i], coldev(mate, x))
    for d in (1, 3, 2):
        give_back(c, bx_recv, coldev(z, on_x[d]))
    act_ref[...] = (summed * sigma).astype(BF16)
    term = jnp.dot(aggregated.astype(F32).T.astype(BF16), grad_rows, preferred_element_type=F32)
    high, wide = wown.shape[1:]
    blocks = [(i * high, j * wide) for i in range(term.shape[0] // high) for j in range(term.shape[1] // wide)]
    for i, (top, left) in enumerate(blocks):
        wown[i] = term[top : top + high, left : left + wide]
    for g, (dx, dy, dc) in enumerate(group[1:]):
        send(
            wown.at[piece_of(on_x[dx], on_y[dy], on_core[dc])], wr1.at[g], w_send.at[0], w_recv.at[0],
            group_device(dx, dy, dc),
        )
    last = NZ - 1
    for zz, sem in [(side, 1), (across, 0), (mates[1], 2), (mates[2], 3), (across, last), (far[0], 4), (far[1], 5), (far[2], 6)]:
        t = zz * NX + (on_x[2] if sem == last else x)
        arrived(bbuf.at[t], bz_recv.at[sem])
        if sem in (0, last):
            for i, mate in reversed(list(enumerate(mates))):
                give_back(t, bx_recv if sem == last else bz_recv.at[4 + i], coldev(mate, x))
        if sem != last:
            for d in (1, 3, 2)[: 2 if sem >= 4 else 3]:
                give_back(t, bz_recv.at[last] if (sem, d) == (0, 2) else bx_recv, coldev(z, on_x[d]))

    place = piece_of(x, y, core)
    arrived(wr1, w_recv.at[0])
    piece = wown[place]
    for g in range(len(group) - 1):
        piece += wr1[g]
    wz[...] = piece
    for g in [ring // 2] + [g for g in range(1, ring) if g != ring // 2]:
        send(wz, wrz.at[g - 1], w_send.at[1], w_recv.at[1], ring_device(g))
    arrived(bbuf.at[pl.ds(0, (NX - 1) * NZ - 1)], bx_recv)

    product_scan(4, lambda i, s: jnp.dot(bbuf[s], vals[i], preferred_element_type=F32))

    for j in (1, 0):
        for i in (1, 0):
            for yy in range(NY):
                qpack[j, i, yy] = sums[tabs[7, tile_of(yy, on_h[i], on_core[j])]]
            if j == 1:
                send(qpack.at[j, i], rq.at[i], q_send, qk_recv.at[i], rowdev(y, h, on_core[1]))
    own = {}
    for i in (1, 0):
        arrived(rq.at[i], qk_recv.at[i])
        for d in range(1, NY):
            yy = on_y[d]
            ys[i, d - 1] = (qpack[0, i, yy].astype(F32) + rq[i, yy].astype(F32)).astype(BF16)
            send(ys.at[i, d - 1], ry.at[i, d - 1], q_send, qy_recv.at[i], rowdev(yy, h, core))
        own[i] = qpack[0, i, y].astype(F32) + rq[i, y].astype(F32)
    arrived(ry.at[1], qy_recv.at[1])
    for d in range(NY - 1):
        own[1] += ry[1, d].astype(F32)
    zh[...] = own[1].astype(BF16)
    send(zh, rzh, q_send, qh_recv, rowdev(y, on_h[1], core))
    arrived(wrz, w_recv.at[1])
    for g in range(ring - 1):
        piece += wrz[g]
    wall[place] = piece * scale
    for g in group[1:]:
        send(wall.at[place], wall.at[place], w_send.at[2], w_recv.at[2], group_device(*g))
    arrived(ry.at[0], qy_recv.at[0])
    for d in range(NY - 1):
        own[0] += ry[0, d].astype(F32)
    waiter(xbuf.at[pl.ds(0, NY * NH * NC - 1)], x_send).wait_send()
    waiter(rx, px_send).wait_send()
    waiter(rz, pz_send).wait_send()
    waiter(bbuf.at[pl.ds(0, NZ * NX - 1)], b_send).wait_send()
    waiter(xbuf.at[pl.ds(0, NH * NY + NH * (NY - 1) + 1)], q_send).wait_send()
    waiter(wr1, w_send.at[0]).wait_send()
    waiter(wrz, w_send.at[1]).wait_send()
    waiter(wr1, w_send.at[2]).wait_send()
    arrived(wr1, w_recv.at[2])
    for i, (top, left) in enumerate(blocks):
        wg_ref[top : top + high, left : left + wide] = wall[i]
    arrived(rzh, qh_recv)
    fg_ref[...] = (own[0] + rzh[...].astype(F32)).T.astype(BF16)


def per_device(features, weight, tile_values, tile_row, tile_col, tile_count, upstream):
    rows, width = features.shape
    hidden = weight.shape[1]
    slots = tile_values.shape[1]
    nodes = rows * lax.axis_size("row") * lax.axis_size("col")
    tile = (T, T)
    group = NX * NY * NC
    ring = NH * NZ
    piece = (8, 128)
    dma = pltpu.SemaphoreType.DMA
    vm = pl.BlockSpec(memory_space=pltpu.VMEM)
    hbm = pl.BlockSpec(memory_space=pl.ANY)
    flops = 2 * 2 * slots * T * T * T
    return pl.pallas_call(
        functools.partial(kernel, 1.0 / math.sqrt(nodes)),
        out_shape=(
            pltpu.VMEM((rows, hidden), BF16),
            pltpu.VMEM((rows, width), BF16),
            pltpu.VMEM((width, hidden), F32),
        ),
        in_specs=[hbm] * 7,
        out_specs=(vm, vm, vm),
        scratch_shapes=[
            pltpu.VMEM(weight.shape, BF16),
            pltpu.VMEM(tile_row.shape, jnp.int32),
            pltpu.VMEM(tile_col.shape, jnp.int32),
            pltpu.VMEM(upstream.shape, BF16),
            pltpu.SMEM(tile_count.shape, jnp.int32),
            pltpu.VMEM((slots,) + tile, BF16),
            pltpu.VMEM((NY * NH * NC,) + tile, BF16),
            pltpu.VMEM((slots + 1,) + tile, BF16),
            pltpu.VMEM((NX, NZ) + tile, BF16),
            pltpu.VMEM((NZ, NX - 1) + tile, BF16),
            pltpu.VMEM((NZ,) + tile, BF16),
            pltpu.VMEM((NZ - 1,) + tile, BF16),
            pltpu.VMEM((NZ * NX,) + tile, BF16),
            pltpu.VMEM((NC, NH, NY) + tile, BF16),
            pltpu.VMEM((NH, NY) + tile, BF16),
            pltpu.VMEM((NH, NY - 1) + tile, BF16),
            pltpu.VMEM((NH, NY - 1) + tile, BF16),
            pltpu.VMEM(tile, BF16),
            pltpu.VMEM(tile, BF16),
            pltpu.VMEM((group,) + piece, F32),
            pltpu.VMEM((group - 1,) + piece, F32),
            pltpu.VMEM(piece, F32),
            pltpu.VMEM((ring - 1,) + piece, F32),
            pltpu.VMEM((group,) + piece, F32),
            pltpu.VMEM((8, slots), jnp.int32),
            pltpu.SMEM((8, slots), jnp.int32),
            dma((8,)),
            dma, dma, dma((NH, NY - 1)), dma,
            dma, dma((NZ,)), dma, dma,
            dma, dma((NZ,)), dma,
            dma, dma((NH,)), dma((NH,)), dma,
            dma((3,)), dma((3,)),
        ],
        compiler_params=pltpu.CompilerParams(
            collective_id=0, has_side_effects=True, vmem_limit_bytes=56 * 1024 * 1024
        ),
        cost_estimate=pl.CostEstimate(flops=flops, bytes_accessed=slots * T * T * 2, transcendentals=rows * hidden),
    )(features, weight, tile_values, tile_row, tile_col, tile_count, upstream)


def solution(mesh):
    in_specs = (
        P(("col", "row"), None),
        P(),
        P("row", "col", None, None),
        P("row", "col"),
        P("row", "col"),
        P("row", "col"),
        P(("row", "col"), None),
    )
    out_specs = (P(("row", "col"), None), P(("col", "row"), None), P())
    return jax.shard_map(
        per_device, mesh=mesh, in_specs=in_specs, out_specs=out_specs, check_vma=False
    )
```

```python
import functools
import math

import jax
import jax.numpy as jnp
from jax import lax
from jax.experimental import pallas as pl
from jax.experimental.pallas import tpu as pltpu
from jax.sharding import PartitionSpec as P

MESH = pl.DeviceIdType.MESH
F32 = jnp.float32
BF16 = jnp.bfloat16
T = 128

NX, NZ, NY, NH, NC = 4, 8, 4, 2, 2
UNROLL = 128


def order_tables(target, source, live, bins):
    slots = target.shape[1]
    lane = lax.broadcasted_iota(jnp.int32, (slots, slots), 1)
    sub = lax.broadcasted_iota(jnp.int32, (slots, slots), 0)
    wide = jnp.where(lane < live, jnp.broadcast_to(target, (slots, slots)), bins)
    key = wide * slots + lane
    tall = wide.T
    tall_key = tall * slots + sub
    rank = jnp.sum((tall_key < key).astype(jnp.int32), axis=0, keepdims=True)
    tall_rank = jnp.broadcast_to(rank, (slots, slots)).T
    placed = tall_rank == lane
    tall_source = jnp.broadcast_to(source, (slots, slots)).T
    perm = jnp.sum(jnp.where(placed, sub, 0), axis=0, keepdims=True)
    src = jnp.sum(jnp.where(placed, tall_source, 0), axis=0, keepdims=True)
    place = jnp.sum(jnp.where(placed, tall, 0), axis=0, keepdims=True)
    before = jnp.sum(jnp.where(tall_rank + 1 == lane, tall, 0), axis=0, keepdims=True)
    first = lax.broadcasted_iota(jnp.int32, (1, slots), 1) == 0
    keep = jnp.where((place == before) & jnp.logical_not(first), 1, 0)
    upto = jnp.sum((tall <= lane).astype(jnp.int32), axis=0, keepdims=True)
    here = jnp.sum((tall == lane).astype(jnp.int32), axis=0, keepdims=True)
    last = jnp.where(here > 0, upto - 1, slots)
    return perm, src, keep, last


def kernel(
    scale,
    feat_hbm, weight_hbm, vals_hbm, row_hbm, col_hbm, count_hbm, up_hbm,
    act_ref, fg_ref, wg_ref,
    weight_ref, row_ref, col_ref, up_ref, count_ref,
    vals, xbuf, sums, pbuf, rx, zs, rz, bbuf, qpack, rq, ys, ry, zh, rzh,
    wown, wr1, wz, wrz, wall,
    tabv, tabs,
    local_sem, x_send, xh_recv, xy_recv, xk_recv, px_send, px_recv, pz_send, pz_recv,
    b_send, bz_recv, bx_recv, q_send, qk_recv, qy_recv, qh_recv,
    w_send, w_recv,
):
    r = lax.axis_index("row")
    c = lax.axis_index("col")
    core, h, y = lax.rem(r, NC), lax.rem(lax.div(r, NC), NH), lax.div(r, NC * NH)
    x, z = lax.rem(c, NX), lax.div(c, NX)
    slots = vals.shape[0]
    on_x = [lax.rem(x + d, NX) for d in range(NX)]
    on_y = [lax.rem(y + d, NY) for d in range(NY)]
    on_h = [h, 1 - h]
    on_core = [core, 1 - core]

    def tile_of(yy, hh, cc):
        return (yy * NH + hh) * NC + cc

    def rowdev(yy, hh, cc):
        return {"row": tile_of(yy, hh, cc), "col": c}

    def coldev(zz, xx):
        return {"row": r, "col": zz * NX + xx}

    group = [(dx, dy, dc) for dx in range(NX) for dy in range(NY) for dc in range(NC)]
    ring = NH * NZ
    spot = h * NZ + z

    def piece_of(xx, yy, cc):
        return (xx * NY + yy) * NC + cc

    def group_device(dx, dy, dc):
        return {"row": tile_of(on_y[dy], h, on_core[dc]), "col": z * NX + on_x[dx]}

    def ring_device(g):
        p = lax.rem(spot + g, ring)
        hh = lax.div(p, NZ)
        return {"row": tile_of(y, hh, core), "col": (p - hh * NZ) * NX + x}

    def send(src, dst, send_sem, recv_sem, device):
        pltpu.make_async_remote_copy(
            src_ref=src, dst_ref=dst, send_sem=send_sem, recv_sem=recv_sem, device_id=device, device_id_type=MESH
        ).start()

    def waiter(ref, sem):
        return pltpu.make_async_remote_copy(
            src_ref=ref, dst_ref=ref, send_sem=sem, recv_sem=sem,
            device_id=rowdev(y, h, on_core[1]), device_id_type=MESH,
        )

    def arrived(ref, sem):
        waiter(ref, sem).wait_recv()

    barrier = pltpu.get_barrier_semaphore()
    peers = [ring_device(g) for g in [ring // 2] + [g for g in range(1, ring) if g != ring // 2]]
    peers += [group_device(*g) for g in group[1:]]
    for peer in peers:
        pl.semaphore_signal(barrier, inc=1, device_id=peer, device_id_type=MESH)
    own_copies = [
        pltpu.make_async_copy(src, dst, local_sem.at[i])
        for i, (src, dst) in enumerate([
            (row_hbm, row_ref), (col_hbm, col_ref), (count_hbm, count_ref), (feat_hbm, xbuf.at[r]),
            (weight_hbm, weight_ref), (up_hbm, up_ref), (vals_hbm.at[0], vals),
        ])
    ]
    for copy in own_copies:
        copy.start()
    own_copies[3].wait()
    pl.semaphore_wait(barrier, len(peers))

    def share(tile, recv_sem, device):
        send(xbuf.at[tile], xbuf.at[tile], x_send, recv_sem, device)

    share(r, xh_recv, rowdev(y, on_h[1], core))
    for d in range(1, NY):
        share(r, xy_recv.at[0, d - 1], rowdev(on_y[d], h, core))
    share(r, xk_recv, rowdev(y, h, on_core[1]))
    for copy in own_copies[:3]:
        copy.wait()
    live = count_ref[0, 0]
    forward = order_tables(row_ref[...], col_ref[...], live, NZ * NX)
    for i, table in enumerate(forward):
        tabv[i : i + 1, :] = table
    backward = order_tables(col_ref[...], row_ref[...], live, NY * NH * NC)
    for i, table in enumerate(backward):
        tabv[4 + i : 5 + i, :] = table
    tabs_copy = pltpu.make_async_copy(tabv, tabs, local_sem.at[7])
    tabs_copy.start()
    sums[slots] = jnp.zeros((T, T), BF16)

    for i in range(NH):
        if i == 1:
            other = tile_of(y, on_h[1], core)
            arrived(xbuf.at[other], xh_recv)
            for d in range(1, NY):
                share(other, xy_recv.at[1, d - 1], rowdev(on_y[d], h, core))
            share(other, xk_recv, rowdev(y, h, on_core[1]))
        for d in (1, 3, 2):
            tile = tile_of(on_y[d], on_h[i], core)
            arrived(xbuf.at[tile], xy_recv.at[i, NY - d - 1])
            share(tile, xk_recv, rowdev(y, h, on_core[1]))
    arrived(xbuf.at[pl.ds(0, NY * NH)], xk_recv)

    tabs_copy.wait()
    for copy in own_copies[4:]:
        copy.wait()

    def product_scan(base, multiply):
        def body(step, total):
            for u in range(UNROLL):
                k = step * UNROLL + u
                keep = tabs[base + 2, k].astype(F32)
                total = total * keep + multiply(tabs[base, k], tabs[base + 1, k])
                sums[k] = total.astype(BF16)
            return total

        lax.fori_loop(0, slots // UNROLL, body, jnp.zeros((T, T), F32))

    product_scan(0, lambda i, s: jnp.dot(vals[i], xbuf[s], preferred_element_type=F32))

    def near(k):
        side = jnp.minimum(z, NZ - 1 - z)
        both = k <= 2 * side
        far = jnp.where(both, (k + 1) // 2, k - side)
        up = jnp.where(both, k % 2 == 1, z < NZ // 2)
        return z + jnp.where(up, far, -far)

    order = [near(k) for k in range(NZ - 1, 0, -1)] + [z]
    for zz in order:
        for d in (1, 3, 2):
            pbuf[on_x[d], zz] = sums[tabs[3, zz * NX + on_x[d]]]
            send(pbuf.at[on_x[d], zz], rx.at[zz, d - 1], px_send, px_recv.at[zz], coldev(z, on_x[d]))
    for o, zz in enumerate(order):
        arrived(rx.at[zz], px_recv.at[zz])
        total = sums[tabs[3, zz * NX + x]].astype(F32)
        for d in range(1, NX):
            total += rx[zz, d - 1].astype(F32)
        if o < NZ - 1:
            zs[zz] = total.astype(BF16)
            slot = lax.rem(zz - z + NZ, NZ) - 1
            send(zs.at[zz], rz.at[slot], pz_send, pz_recv, coldev(zz, x))
    arrived(rz, pz_recv)
    for o in range(NZ - 1):
        total += rz[o].astype(F32)
    aggregated = total.astype(BF16)

    weight = weight_ref[...]
    summed = jnp.dot(aggregated, weight, preferred_element_type=F32)
    sigma = jax.nn.sigmoid(summed)
    slope = sigma * (1.0 + summed * (1.0 - sigma))
    grad_rows = (up_ref[...].astype(F32) * slope).astype(BF16)
    back = lax.dot_general(weight, grad_rows, (((1,), (1,)), ((), ())), preferred_element_type=F32)
    bbuf[c] = back.astype(BF16)

    side = z + 1 - 2 * lax.rem(z, 2)
    turn = 2 - 4 * lax.rem(lax.div(z, 2), 2)
    mates = [side, z + turn, side + turn]
    across = lax.rem(z + NZ // 2, NZ)
    far = [lax.rem(mate + NZ // 2, NZ) for mate in mates]

    def give_back(t, recv_sem, device):
        send(bbuf.at[t], bbuf.at[t], b_send, recv_sem, device)

    give_back(c, bz_recv.at[0], coldev(across, x))
    for i, mate in enumerate(mates):
        give_back(c, bz_recv.at[1 + i], coldev(mate, x))
    for d in (1, 3, 2):
        give_back(c, bx_recv, coldev(z, on_x[d]))
    act_ref[...] = (summed * sigma).astype(BF16)
    term = jnp.dot(aggregated.astype(F32).T.astype(BF16), grad_rows, preferred_element_type=F32)
    high, wide = wown.shape[1:]
    blocks = [(i * high, j * wide) for i in range(term.shape[0] // high) for j in range(term.shape[1] // wide)]
    for i, (top, left) in enumerate(blocks):
        wown[i] = term[top : top + high, left : left + wide]
    for g, (dx, dy, dc) in enumerate(group[1:]):
        send(
            wown.at[piece_of(on_x[dx], on_y[dy], on_core[dc])], wr1.at[g], w_send.at[0], w_recv.at[0],
            group_device(dx, dy, dc),
        )
    last = NZ - 1
    for zz, sem in [(side, 1), (across, 0), (mates[1], 2), (mates[2], 3), (across, last), (far[0], 4), (far[1], 5), (far[2], 6)]:
        t = zz * NX + (on_x[2] if sem == last else x)
        arrived(bbuf.at[t], bz_recv.at[sem])
        if sem in (0, last):
            for i, mate in reversed(list(enumerate(mates))):
                give_back(t, bx_recv if sem == last else bz_recv.at[4 + i], coldev(mate, x))
        if sem != last:
            for d in (1, 3, 2)[: 2 if sem >= 4 else 3]:
                give_back(t, bz_recv.at[last] if (sem, d) == (0, 2) else bx_recv, coldev(z, on_x[d]))

    place = piece_of(x, y, core)
    arrived(wr1, w_recv.at[0])
    piece = wown[place]
    for g in range(len(group) - 1):
        piece += wr1[g]
    wz[...] = piece
    for g in [ring // 2] + [g for g in range(1, ring) if g != ring // 2]:
        send(wz, wrz.at[g - 1], w_send.at[1], w_recv.at[1], ring_device(g))
    arrived(bbuf.at[pl.ds(0, (NX - 1) * NZ - 1)], bx_recv)

    product_scan(4, lambda i, s: jnp.dot(bbuf[s], vals[i], preferred_element_type=F32))

    for i in (1, 0):
        for yy in range(NY):
            qpack[i, yy] = sums[tabs[7, tile_of(yy, on_h[i], on_core[1])]]
        send(qpack.at[i], rq.at[i], q_send, qk_recv.at[i], rowdev(y, h, on_core[1]))
    def mine(i, yy):
        return sums[tabs[7, tile_of(yy, on_h[i], core)]].astype(F32)

    own = {}
    for i in (1, 0):
        arrived(rq.at[i], qk_recv.at[i])
        for d in range(1, NY):
            yy = on_y[d]
            ys[i, d - 1] = (mine(i, yy) + rq[i, yy].astype(F32)).astype(BF16)
            send(ys.at[i, d - 1], ry.at[i, d - 1], q_send, qy_recv.at[i], rowdev(yy, h, core))
        own[i] = mine(i, y) + rq[i, y].astype(F32)
    arrived(ry.at[1], qy_recv.at[1])
    for d in range(NY - 1):
        own[1] += ry[1, d].astype(F32)
    zh[...] = own[1].astype(BF16)
    send(zh, rzh, q_send, qh_recv, rowdev(y, on_h[1], core))
    arrived(wrz, w_recv.at[1])
    for g in range(ring - 1):
        piece += wrz[g]
    wall[place] = piece * scale
    for g in group[1:]:
        send(wall.at[place], wall.at[place], w_send.at[2], w_recv.at[2], group_device(*g))
    arrived(ry.at[0], qy_recv.at[0])
    for d in range(NY - 1):
        own[0] += ry[0, d].astype(F32)
    waiter(xbuf.at[pl.ds(0, NY * NH * NC - 1)], x_send).wait_send()
    waiter(rx, px_send).wait_send()
    waiter(rz, pz_send).wait_send()
    waiter(bbuf.at[pl.ds(0, NZ * NX - 1)], b_send).wait_send()
    waiter(xbuf.at[pl.ds(0, NH * NY + NH * (NY - 1) + 1)], q_send).wait_send()
    waiter(wr1, w_send.at[0]).wait_send()
    waiter(wrz, w_send.at[1]).wait_send()
    waiter(wr1, w_send.at[2]).wait_send()
    arrived(wr1, w_recv.at[2])
    for i, (top, left) in enumerate(blocks):
        wg_ref[top : top + high, left : left + wide] = wall[i]
    arrived(rzh, qh_recv)
    fg_ref[...] = (own[0] + rzh[...].astype(F32)).T.astype(BF16)


def per_device(features, weight, tile_values, tile_row, tile_col, tile_count, upstream):
    rows, width = features.shape
    hidden = weight.shape[1]
    slots = tile_values.shape[1]
    nodes = rows * lax.axis_size("row") * lax.axis_size("col")
    tile = (T, T)
    group = NX * NY * NC
    ring = NH * NZ
    piece = (8, 128)
    dma = pltpu.SemaphoreType.DMA
    vm = pl.BlockSpec(memory_space=pltpu.VMEM)
    hbm = pl.BlockSpec(memory_space=pl.ANY)
    flops = 2 * 2 * slots * T * T * T
    return pl.pallas_call(
        functools.partial(kernel, 1.0 / math.sqrt(nodes)),
        out_shape=(
            pltpu.VMEM((rows, hidden), BF16),
            pltpu.VMEM((rows, width), BF16),
            pltpu.VMEM((width, hidden), F32),
        ),
        in_specs=[hbm] * 7,
        out_specs=(vm, vm, vm),
        scratch_shapes=[
            pltpu.VMEM(weight.shape, BF16),
            pltpu.VMEM(tile_row.shape, jnp.int32),
            pltpu.VMEM(tile_col.shape, jnp.int32),
            pltpu.VMEM(upstream.shape, BF16),
            pltpu.SMEM(tile_count.shape, jnp.int32),
            pltpu.VMEM((slots,) + tile, BF16),
            pltpu.VMEM((NY * NH * NC,) + tile, BF16),
            pltpu.VMEM((slots + 1,) + tile, BF16),
            pltpu.VMEM((NX, NZ) + tile, BF16),
            pltpu.VMEM((NZ, NX - 1) + tile, BF16),
            pltpu.VMEM((NZ,) + tile, BF16),
            pltpu.VMEM((NZ - 1,) + tile, BF16),
            pltpu.VMEM((NZ * NX,) + tile, BF16),
            pltpu.VMEM((NH, NY) + tile, BF16),
            pltpu.VMEM((NH, NY) + tile, BF16),
            pltpu.VMEM((NH, NY - 1) + tile, BF16),
            pltpu.VMEM((NH, NY - 1) + tile, BF16),
            pltpu.VMEM(tile, BF16),
            pltpu.VMEM(tile, BF16),
            pltpu.VMEM((group,) + piece, F32),
            pltpu.VMEM((group - 1,) + piece, F32),
            pltpu.VMEM(piece, F32),
            pltpu.VMEM((ring - 1,) + piece, F32),
            pltpu.VMEM((group,) + piece, F32),
            pltpu.VMEM((8, slots), jnp.int32),
            pltpu.SMEM((8, slots), jnp.int32),
            dma((8,)),
            dma, dma, dma((NH, NY - 1)), dma,
            dma, dma((NZ,)), dma, dma,
            dma, dma((NZ,)), dma,
            dma, dma((NH,)), dma((NH,)), dma,
            dma((3,)), dma((3,)),
        ],
        compiler_params=pltpu.CompilerParams(
            collective_id=0, has_side_effects=True, vmem_limit_bytes=56 * 1024 * 1024
        ),
        cost_estimate=pl.CostEstimate(flops=flops, bytes_accessed=slots * T * T * 2, transcendentals=rows * hidden),
    )(features, weight, tile_values, tile_row, tile_col, tile_count, upstream)


def solution(mesh):
    in_specs = (
        P(("col", "row"), None),
        P(),
        P("row", "col", None, None),
        P("row", "col"),
        P("row", "col"),
        P("row", "col"),
        P(("row", "col"), None),
    )
    out_specs = (P(("row", "col"), None), P(("col", "row"), None), P())
    return jax.shard_map(
        per_device, mesh=mesh, in_specs=in_specs, out_specs=out_specs, check_vma=False
    )
```
